32 devices in a mesh: slab: 4 (over y, core), grp: 8 (over z, x).
Axes of the slice: x: 2, y: 2, z: 4, core: 2. Of those that a mesh axis runs over, the one named last changes fastest.
Arguments:
- node_feats: bfloat16 [262144, 128], P(('slab', 'grp')), may hold values from -6 to 6
- cotangent: bfloat16 [262144, 128], P(('slab', 'grp')), may hold values from -6 to 6
- fine_adjacency: bfloat16 [4096, 64, 768], P(('slab', 'grp')), may hold values from -0.21875 to 0.21875
- fine_columns: int32 [4096, 12], P(('slab', 'grp')), may hold values from 0 to 143, as said below
- pool_one: bfloat16 [512, 64, 512], P(('slab', 'grp')), may hold values from -0.25 to 0.25
- pool_one_columns: int32 [512, 8], P(('slab', 'grp')), may hold values from 0 to 127
- count_one: int32 [32], P(('slab', 'grp')), may hold values from 256 to 1024, as said below
- owner_one: int32 [32768], P(('slab', 'grp')), may hold values from 0 to 4095, as said below
- adjacency_one: bfloat16 [256, 64, 512], P(('slab', 'grp')), may hold values from -0.25 to 0.25
- columns_one: int32 [256, 8], P(('slab', 'grp')), may hold values from 0 to 63
- pool_two: bfloat16 [128, 64, 512], P(('slab', 'grp')), may hold values from -0.25 to 0.25
- pool_two_columns: int32 [128, 8], P(('slab', 'grp')), may hold values from 0 to 7
- count_two: int32 [32], P(('slab', 'grp')), may hold values from 64 to 256, as said below
- owner_two: int32 [8192], P(('slab', 'grp')), may hold values from 0 to 1023, as said below
- adjacency_two: bfloat16 [64, 64, 512], P(('slab', 'grp')), may hold values from -0.25 to 0.25
- columns_two: int32 [64, 8], P(('slab', 'grp')), may hold values from 0 to 15
- weight_in: bfloat16 [3, 256, 128], replicated, may hold values from -0.375 to 0.375
- weight_out: bfloat16 [3, 128, 128], replicated, may hold values from -0.5 to 0.5
- biases: float32 [3, 128], replicated, may hold values from -3 to 3
Outputs:
- node_out: bfloat16 [262144, 128], P(('slab', 'grp'))
- grad_feats: bfloat16 [262144, 128], P(('slab', 'grp'))
- grad_weight_in: float32 [3, 256, 128], replicated
- grad_weight_out: float32 [3, 128, 128], replicated
- grad_biases: float32 [3, 128], replicated
The draws below stay inside these ranges and needn't reach their ends.
Inputs may be any that keep to these rules, and one draw needn't show every extreme that they name: `fine_columns`: row block r of a device reads blocks r to r + 16 of its extended rows. `count_one`: the 8 counts of one slab sum to 4096, and one of them equals 1024. `owner_one`: the live slots of a device are its first count_one slots. In one slab the live slots' values take each value below 4096 exactly once; value v names row v % 512 of device v // 512 of the slab. At most 128 live slots of one device name rows of one device, and in every slab some device has exactly that many for every device. Values of other slots are unused. `count_two`: the 8 counts of one slab sum to 1024, and one of them equals 256. `owner_two`: the live slots of a device are its first count_two slots. In one slab the live slots' values take each value below 1024 exactly once; value v names row v % 128 of device v // 128 of the slab. At most 32 live slots of one device name rows of one device, and in every slab some device has exactly that many for every device. Values of other slots are unused.
All inputs are finite; a program needn't handle non-finite values.
Results may differ from the reference program's by a relative error of at most 0.012.
Values may be sent and summed in bfloat16 or wider, within the bound.
No kernel may reach another device: no remote copies, remote signals or barrier semaphores. Data moves between devices by JAX's collectives and lax.ppermute only.
A program may use at most 320 MiB of HBM per device.

```python
import math
import jax
import jax.numpy as jnp
from jax import lax

H = 128
BLK = 64
F_DEV = 8192
HALO = 512
K0 = 12
K1 = 8
K2 = 8
KR = 8
C1 = 1024
B1 = 512
C2 = 256
B2 = 128
NODES = 262144
N_SLAB = 4
N_GRP = 8


def level_routes(key, slot_total, balance):

    def one_slab(slab_key):
        key_list = jax.random.split(slab_key, 5)
        shuffled = jax.random.permutation(key_list[0], N_GRP)
        position = jnp.arange(N_GRP, dtype=jnp.int32)
        amounts = jax.random.randint(key_list[1], (N_GRP,), 0, balance // 2 + 1)
        parity = jnp.mod(position - 3, 2)
        first_of = position - parity
        paired = (position >= 3) & (first_of + 1 <= N_GRP - 1)
        signs = 1 - 2 * parity
        shared = amounts[jnp.clip((first_of - 3) // 2, 0, N_GRP - 1)]
        deltas = jnp.where(position == 0, balance, jnp.where(position <= 2, -(balance // 2), jnp.where(paired, signs * shared, 0)))
        counts = jnp.zeros((N_GRP,), jnp.int32).at[shuffled].set((balance + deltas).astype(jnp.int32))
        starts = jnp.cumsum(counts) - counts
        within = jnp.arange(slot_total, dtype=jnp.int32)
        live_mask = within[None, :] < counts[:, None]
        global_rank = starts[:, None] + within[None, :]
        rotation = jax.random.randint(key_list[2], (), 0, N_GRP)
        owners = jnp.mod(global_rank + rotation, N_GRP)
        depth = jnp.clip(global_rank // N_GRP, 0, balance - 1)
        shuffles = jax.vmap(lambda sub_key: jax.random.permutation(sub_key, balance))(jax.random.split(key_list[3], N_GRP))
        owner_rows = owners * balance + shuffles[owners, depth]
        spare_rows = jax.random.randint(key_list[4], (N_GRP, slot_total), 0, N_GRP * balance)
        return (counts, jnp.where(live_mask, owner_rows, spare_rows).astype(jnp.int32).reshape(-1))
    counts, owners = jax.vmap(one_slab)(jax.random.split(key, N_SLAB))
    return (counts.reshape(-1).astype(jnp.int32), owners.reshape(-1).astype(jnp.int32))


def draw_fine_columns(key, part):
    block_total = N_SLAB * N_GRP * (F_DEV // BLK)
    reach = HALO // BLK
    local_rows = jnp.arange(block_total, dtype=jnp.int32) % (F_DEV // BLK)
    offsets = jax.random.randint(jax.random.fold_in(key, 5), (block_total, K0), -reach, reach + 1)
    return (local_rows[:, None] + reach + offsets).astype(jnp.int32)


def draw_count_one(key, part):
    return level_routes(jax.random.fold_in(key, 11), C1, B1)[0]


def draw_owner_one(key, part):
    return level_routes(jax.random.fold_in(key, 11), C1, B1)[1]


def draw_count_two(key, part):
    return level_routes(jax.random.fold_in(key, 22), C2, B2)[0]


def draw_owner_two(key, part):
    return level_routes(jax.random.fold_in(key, 22), C2, B2)[1]


def place_ends(values, rng, low, largest):
    extent = values.shape
    spot = [jax.random.randint(jax.random.fold_in(rng, axis), (), 0, extent[axis]) for axis in range(len(extent))]
    values = values.at[tuple(spot)].set(low)
    longest = extent.index(max(extent))
    spot[longest] = (spot[longest] + 1) % extent[longest]
    return values.at[tuple(spot)].set(largest)


def block_levels(key, extent, cuts, smallest, high):
    factor_of = 1.0
    for axis_at, parts in cuts:
        steps = jax.random.uniform(jax.random.fold_in(jax.random.fold_in(key, 6), axis_at), (parts,), jnp.float32, smallest / len(cuts), high / len(cuts))
        factor_of = factor_of * jnp.repeat(jnp.exp(steps), extent[axis_at] // parts).reshape((-1,) + (1,) * (len(extent) - 1 - axis_at))
    return factor_of


def noise(own_key, shape, scale, most, cuts=(), kind=jnp.bfloat16):
    drawn = scale * jax.random.normal(own_key, shape, jnp.float32)
    if cuts:
        drawn = drawn * block_levels(own_key, shape, cuts, -0.22, 0.18)
    return jnp.clip(drawn, -most, most).astype(kind)


def setup_inputs(seed: int = 0) -> dict:
    seeds = jax.random.split(jax.random.key(seed), 20)
    return {
        "node_feats": noise(seeds[0], (NODES, H), 1.0, 6.0, ((0, 32),)),
        "cotangent": noise(seeds[1], (NODES, H), 1.0, 6.0, ((0, 32),)),
        "fine_adjacency": noise(seeds[2], (N_SLAB * N_GRP * (F_DEV // BLK), BLK, K0 * BLK), (K0 * BLK) ** -0.5, 0.21875, ((0, 32),)),
        "fine_columns": draw_fine_columns(jax.random.fold_in(seeds[19], 71), 0),
        "pool_one": noise(seeds[4], (N_SLAB * N_GRP * (C1 // BLK), BLK, KR * BLK), (KR * BLK) ** -0.5, 0.25, ((0, 32),)),
        "pool_one_columns": place_ends(jax.random.randint(seeds[5], (N_SLAB * N_GRP * (C1 // BLK), KR), 0, F_DEV // BLK), jax.random.fold_in(seeds[5], 1), 0, (F_DEV // BLK) - 1).astype(jnp.int32),
        "count_one": draw_count_one(jax.random.fold_in(seeds[19], 71), 0),
        "owner_one": draw_owner_one(jax.random.fold_in(seeds[19], 71), 0),
        "adjacency_one": noise(seeds[8], (N_SLAB * N_GRP * (B1 // BLK), BLK, K1 * BLK), (K1 * BLK) ** -0.5, 0.25, ((0, 32),)),
        "columns_one": place_ends(jax.random.randint(seeds[9], (N_SLAB * N_GRP * (B1 // BLK), K1), 0, N_GRP * (B1 // BLK)), jax.random.fold_in(seeds[9], 1), 0, (N_GRP * (B1 // BLK)) - 1).astype(jnp.int32),
        "pool_two": noise(seeds[10], (N_SLAB * N_GRP * (C2 // BLK), BLK, KR * BLK), (KR * BLK) ** -0.5, 0.25, ((0, 32),)),
        "pool_two_columns": place_ends(jax.random.randint(seeds[11], (N_SLAB * N_GRP * (C2 // BLK), KR), 0, B1 // BLK), jax.random.fold_in(seeds[11], 1), 0, (B1 // BLK) - 1).astype(jnp.int32),
        "count_two": draw_count_two(jax.random.fold_in(seeds[19], 71), 0),
        "owner_two": draw_owner_two(jax.random.fold_in(seeds[19], 71), 0),
        "adjacency_two": noise(seeds[14], (N_SLAB * N_GRP * (B2 // BLK), BLK, K2 * BLK), (K2 * BLK) ** -0.5, 0.25, ((0, 32),)),
        "columns_two": place_ends(jax.random.randint(seeds[15], (N_SLAB * N_GRP * (B2 // BLK), K2), 0, N_GRP * (B2 // BLK)), jax.random.fold_in(seeds[15], 1), 0, (N_GRP * (B2 // BLK)) - 1).astype(jnp.int32),
        "weight_in": noise(seeds[16], (3, 2 * H, H), (2 * H) ** -0.5, 0.375),
        "weight_out": noise(seeds[17], (3, H, H), H ** -0.5, 0.5),
        "biases": noise(seeds[18], (3, H), 0.5, 3.0, (), jnp.float32),
    }


HIGHEST_PRECISION = lax.Precision.HIGHEST

def device_map(function, *arrays):
    return lax.map(lambda packed: function(*packed), arrays)

def block_apply(blocks, columns, context):
    block_count, block_rows, span = blocks.shape
    feature = context.shape[1]
    tiles = context.reshape(-1, block_rows, feature)
    picked = tiles[columns].reshape(block_count, span, feature)
    product = jnp.einsum('rij,rjh->rih', blocks.astype(jnp.float32), picked.astype(jnp.float32), precision=HIGHEST_PRECISION)
    return product.reshape(block_count * block_rows, feature)

def block_transpose(blocks, columns, row_grads, targets):
    block_count, block_rows, span = blocks.shape
    feature = row_grads.shape[1]
    pieces = row_grads.reshape(block_count, block_rows, feature)
    spread = jnp.einsum('rij,rih->rjh', blocks.astype(jnp.float32), pieces.astype(jnp.float32), precision=HIGHEST_PRECISION)
    spread = spread.reshape(block_count * columns.shape[1], block_rows, feature)
    summed = jax.ops.segment_sum(spread, columns.reshape(-1), num_segments=targets)
    return summed.reshape(targets * block_rows, feature)

def restrict(blocks, columns, source, live_mask):
    pooled = block_apply(blocks, columns, source)
    return jnp.where(live_mask[:, None], pooled, 0.0).astype(jnp.bfloat16)

def layer_forward(node_rows, message, weight_in, weight_out, bias_row):
    joined = jnp.concatenate([node_rows, message], axis=1)
    pre_act = jnp.dot(joined, weight_in, preferred_element_type=jnp.float32) + bias_row
    hidden = jax.nn.silu(pre_act).astype(jnp.bfloat16)
    result = node_rows.astype(jnp.float32) + jnp.dot(hidden, weight_out, preferred_element_type=jnp.float32)
    return (result.astype(jnp.bfloat16), pre_act, hidden)

def layer_backward(cotan_rows, node_rows, message, hidden, pre_act, weight_in, weight_out, blocks, columns, targets):
    grad_low = cotan_rows.astype(jnp.bfloat16)
    delta_out = lax.dot_general(hidden, grad_low, (((0,), (0,)), ((), ())), preferred_element_type=jnp.float32)
    grad_hidden = lax.dot_general(grad_low, weight_out, (((1,), (1,)), ((), ())), preferred_element_type=jnp.float32)
    sigmoid_pre = jax.nn.sigmoid(pre_act)
    grad_pre = grad_hidden * sigmoid_pre * (1.0 + pre_act * (1.0 - sigmoid_pre))
    grad_pre_low = grad_pre.astype(jnp.bfloat16)
    delta_bias = lax.optimization_barrier(jnp.sum(grad_pre, axis=0))
    joined = jnp.concatenate([node_rows, message], axis=1)
    delta_in = lax.dot_general(joined, grad_pre_low, (((0,), (0,)), ((), ())), preferred_element_type=jnp.float32)
    grad_joined = lax.dot_general(grad_pre_low, weight_in, (((1,), (1,)), ((), ())), preferred_element_type=jnp.float32)
    feature = node_rows.shape[1]
    grad_rows = cotan_rows + grad_joined[:, :feature]
    grad_message = grad_joined[:, feature:].astype(jnp.bfloat16)
    grad_context = block_transpose(blocks, columns, grad_message, targets)
    return ((delta_in, delta_out, delta_bias), grad_rows, grad_context)

def pick_slots(table, owners, live_mask):
    taken = jnp.take(table, jnp.clip(owners, 0, table.shape[0] - 1), axis=0)
    return jnp.where(live_mask[..., None], taken, jnp.zeros_like(taken))

def slab_pass(items, weight_in, weight_out, biases):
    node_feats, cotangent, fine_adjacency, fine_columns, pool_one, pool_one_columns, count_one, owner_one, adjacency_one, columns_one, pool_two, pool_two_columns, count_two, owner_two, adjacency_two, columns_two = items
    zero_rim = jnp.zeros((1, HALO, H), jnp.bfloat16)
    before = jnp.concatenate([zero_rim, node_feats[:-1, F_DEV - HALO:]], axis=0)
    after = jnp.concatenate([node_feats[1:, :HALO], zero_rim], axis=0)
    extended = jnp.concatenate([before, node_feats, after], axis=1)

    def fine_message(blocks, columns, context):
        return block_apply(blocks, columns, context).astype(jnp.bfloat16)
    message0 = device_map(fine_message, fine_adjacency, fine_columns, extended)
    result0, pre_act0, hidden0 = device_map(lambda node_rows, message: layer_forward(node_rows, message, weight_in[0], weight_out[0], biases[0]), node_feats, message0)
    live_one = jnp.arange(C1)[None, :] < count_one[:, None]
    coarse_one = device_map(restrict, pool_one, pool_one_columns, result0, live_one)
    target_one = jnp.where(live_one, owner_one, N_GRP * B1).reshape(-1)
    whole_one = jnp.zeros((N_GRP * B1, H), jnp.bfloat16).at[target_one].set(coarse_one.reshape(-1, H), mode='drop')
    message_one = device_map(lambda blocks, columns: fine_message(blocks, columns, whole_one), adjacency_one, columns_one)
    own_one = whole_one.reshape(N_GRP, B1, H)
    result1, pre_act1, hidden1 = device_map(lambda node_rows, message: layer_forward(node_rows, message, weight_in[1], weight_out[1], biases[1]), own_one, message_one)
    live_two = jnp.arange(C2)[None, :] < count_two[:, None]
    coarse_two = device_map(restrict, pool_two, pool_two_columns, result1, live_two)
    target_two = jnp.where(live_two, owner_two, N_GRP * B2).reshape(-1)
    whole_two = jnp.zeros((N_GRP * B2, H), jnp.bfloat16).at[target_two].set(coarse_two.reshape(-1, H), mode='drop')
    message_two = device_map(lambda blocks, columns: fine_message(blocks, columns, whole_two), adjacency_two, columns_two)
    own_two = whole_two.reshape(N_GRP, B2, H)
    result2, pre_act2, hidden2 = device_map(lambda node_rows, message: layer_forward(node_rows, message, weight_in[2], weight_out[2], biases[2]), own_two, message_two)
    back_two = pick_slots(result2.reshape(-1, H), owner_two, live_two)

    def lift_one(blocks, columns, spread, base):
        return (base.astype(jnp.float32) + block_transpose(blocks, columns, spread, B1 // BLK)).astype(jnp.bfloat16)

    def lift_zero(blocks, columns, spread, base):
        return (base.astype(jnp.float32) + block_transpose(blocks, columns, spread, F_DEV // BLK)).astype(jnp.bfloat16)
    up_one = device_map(lift_one, pool_two, pool_two_columns, back_two, result1)
    back_one = pick_slots(up_one.reshape(-1, H), owner_one, live_one)
    node_out = device_map(lift_zero, pool_one, pool_one_columns, back_one, result0)
    grad_slots_one = device_map(restrict, pool_one, pool_one_columns, cotangent, live_one)
    grad_up_one = jnp.zeros((N_GRP * B1, H), jnp.bfloat16).at[target_one].set(grad_slots_one.reshape(-1, H), mode='drop').reshape(N_GRP, B1, H)
    grad_slots_two = device_map(restrict, pool_two, pool_two_columns, grad_up_one, live_two)
    grad_out_two = jnp.zeros((N_GRP * B2, H), jnp.bfloat16).at[target_two].set(grad_slots_two.reshape(-1, H), mode='drop').reshape(N_GRP, B2, H)
    sums_two, grad_rows_two, grad_ctx_two = device_map(lambda cotan_rows, node_rows, message, hidden, pre_act, blocks, columns: layer_backward(cotan_rows.astype(jnp.float32), node_rows, message, hidden, pre_act, weight_in[2], weight_out[2], blocks, columns, N_GRP * B2 // BLK), grad_out_two, own_two, message_two, hidden2, pre_act2, adjacency_two, columns_two)
    grad_own_two = grad_rows_two + lax.optimization_barrier(jnp.sum(grad_ctx_two, axis=0)).reshape(N_GRP, B2, H)
    grad_coarse_two = pick_slots(grad_own_two.reshape(-1, H).astype(jnp.bfloat16), owner_two, live_two)
    grad_out_one = device_map(lambda base, blocks, columns, spread: base.astype(jnp.float32) + block_transpose(blocks, columns, spread, B1 // BLK), grad_up_one, pool_two, pool_two_columns, grad_coarse_two)
    sums_one, grad_rows_one, grad_ctx_one = device_map(lambda cotan_rows, node_rows, message, hidden, pre_act, blocks, columns: layer_backward(cotan_rows, node_rows, message, hidden, pre_act, weight_in[1], weight_out[1], blocks, columns, N_GRP * B1 // BLK), grad_out_one, own_one, message_one, hidden1, pre_act1, adjacency_one, columns_one)
    grad_own_one = grad_rows_one + lax.optimization_barrier(jnp.sum(grad_ctx_one, axis=0)).reshape(N_GRP, B1, H)
    grad_coarse_one = pick_slots(grad_own_one.reshape(-1, H).astype(jnp.bfloat16), owner_one, live_one)
    grad_out_zero = device_map(lambda base, blocks, columns, spread: base.astype(jnp.float32) + block_transpose(blocks, columns, spread, F_DEV // BLK), cotangent, pool_one, pool_one_columns, grad_coarse_one)
    sums_zero, grad_rows_zero, grad_ctx_zero = device_map(lambda cotan_rows, node_rows, message, hidden, pre_act, blocks, columns: layer_backward(cotan_rows, node_rows, message, hidden, pre_act, weight_in[0], weight_out[0], blocks, columns, (F_DEV + 2 * HALO) // BLK), grad_out_zero, node_feats, message0, hidden0, pre_act0, fine_adjacency, fine_columns)
    zero_grads = jnp.zeros((1, HALO, H), jnp.float32)
    from_next = jnp.concatenate([grad_ctx_zero[1:, :HALO], zero_grads], axis=0)
    from_prev = jnp.concatenate([zero_grads, grad_ctx_zero[:-1, HALO + F_DEV:]], axis=0)
    middle = grad_rows_zero + grad_ctx_zero[:, HALO:HALO + F_DEV]
    middle = middle.at[:, :HALO].add(from_prev).at[:, F_DEV - HALO:].add(from_next)
    grad_feats = middle.astype(jnp.bfloat16)
    stack_in = jnp.stack([lax.optimization_barrier(jnp.sum(sums_zero[0], axis=0)), lax.optimization_barrier(jnp.sum(sums_one[0], axis=0)), lax.optimization_barrier(jnp.sum(sums_two[0], axis=0))])
    stack_out = jnp.stack([lax.optimization_barrier(jnp.sum(sums_zero[1], axis=0)), lax.optimization_barrier(jnp.sum(sums_one[1], axis=0)), lax.optimization_barrier(jnp.sum(sums_two[1], axis=0))])
    stack_bias = jnp.stack([lax.optimization_barrier(jnp.sum(sums_zero[2], axis=0)), lax.optimization_barrier(jnp.sum(sums_one[2], axis=0)), lax.optimization_barrier(jnp.sum(sums_two[2], axis=0))])
    return (node_out, grad_feats, stack_in, stack_out, stack_bias)

def reference(node_feats, cotangent, fine_adjacency, fine_columns, pool_one, pool_one_columns, count_one, owner_one, adjacency_one, columns_one, pool_two, pool_two_columns, count_two, owner_two, adjacency_two, columns_two, weight_in, weight_out, biases):

    def split_slab(array):
        return array.reshape((N_SLAB, N_GRP, -1) + array.shape[1:])
    items = (split_slab(node_feats), split_slab(cotangent), split_slab(fine_adjacency), split_slab(fine_columns), split_slab(pool_one), split_slab(pool_one_columns), count_one.reshape(N_SLAB, N_GRP), split_slab(owner_one), split_slab(adjacency_one), split_slab(columns_one), split_slab(pool_two), split_slab(pool_two_columns), count_two.reshape(N_SLAB, N_GRP), split_slab(owner_two), split_slab(adjacency_two), split_slab(columns_two))
    outcome = lax.map(lambda packed: slab_pass(packed, weight_in, weight_out, biases), items)
    inv_root = 1.0 / math.sqrt(NODES)
    return (outcome[0].reshape(-1, H), outcome[1].reshape(-1, H), lax.optimization_barrier(jnp.sum(outcome[2], axis=0)) * inv_root, lax.optimization_barrier(jnp.sum(outcome[3], axis=0)) * inv_root, lax.optimization_barrier(jnp.sum(outcome[4], axis=0)) * inv_root)
```

```python
import functools
import math

import jax
import jax.numpy as jnp
from jax import lax
from jax.experimental import pallas as pl
from jax.experimental.pallas import tpu as pltpu
from jax.sharding import PartitionSpec as P

BF = jnp.bfloat16
F32 = jnp.float32
HALO = 512
BLK = 64
CHUNK = 8
VMEM_LIMIT = 56 * 1024 * 1024

VM = pl.BlockSpec(memory_space=pltpu.VMEM)
SM = pl.BlockSpec(memory_space=pltpu.SMEM)


def params():
    return pltpu.CompilerParams(vmem_limit_bytes=VMEM_LIMIT)


def cost(flops, nbytes):
    return pl.CostEstimate(flops=int(flops), bytes_accessed=int(nbytes), transcendentals=0)


def dot(a, b):
    return jnp.dot(a, b, preferred_element_type=F32)


def dot_nt(a, b):
    return lax.dot_general(a, b, (((1,), (1,)), ((), ())), preferred_element_type=F32)


def dot_tn(a, b):
    return lax.dot_general(a, b, (((0,), (0,)), ((), ())), preferred_element_type=F32)


def iota(shape, dim):
    return lax.broadcasted_iota(jnp.int32, shape, dim)


def as_ones(mask):
    return jnp.where(mask, 1.0, 0.0).astype(BF)


def tile_at(ref, index):
    return ref[pl.ds(pl.multiple_of(index * BLK, BLK), BLK), :]


def apply_row(block, cols, r, count, ref, shift=0):
    picked = jnp.concatenate([tile_at(ref, cols[r, i] - shift) for i in range(count)], axis=0)
    return dot(block, picked)


def spread_row(block, cols, r, count, rows, acc):
    spread = dot_tn(block, rows)
    for i in range(count):
        at = pl.ds(pl.multiple_of(cols[r, i] * BLK, BLK), BLK)
        acc[at, :] += spread[i * BLK : (i + 1) * BLK]


def place_matrix(row_table, first, count):
    n = row_table.shape[1]
    return as_ones(row_table == iota((count, n), 0) + first)


def prep_kernel(count, cols, owner_ref, pool, cot, place_out, table_out, packed_out, slots_scr, *, groups, balance):
    slots = owner_ref.shape[1]
    cap = slots // groups
    k = cols.shape[1]
    for q in range(pool.shape[0]):
        slots_scr[q * BLK : (q + 1) * BLK, :] = apply_row(pool[q], cols, q, k, cot).astype(BF)
    owner = owner_ref[...]
    live = iota((1, slots), 1) < count[0]
    rows = max(16, groups)
    target = iota((rows, slots), 0)
    low = target * balance
    hit = (owner >= low) & (owner < low + balance) & live
    onehot = jnp.where(hit, 1.0, 0.0)
    upper = as_ones(iota((slots, slots), 0) <= iota((slots, slots), 1))
    running = dot(onehot.astype(BF), upper)
    rank = jnp.sum(onehot * running, axis=0, keepdims=True) - 1.0
    base = jnp.sum(jnp.where(hit, target * cap, 0).astype(F32), axis=0, keepdims=True)
    start = jnp.sum(jnp.where(hit, low, 0).astype(F32), axis=0, keepdims=True)
    place = jnp.where(live, (base + rank).astype(jnp.int32), slots)
    place_out[...] = place
    local = owner - start.astype(jnp.int32) + 1
    kind = iota((rows, slots), 0)
    parts = jnp.where(kind == 0, local >> 5, jnp.where(kind == 1, local & 31, 0)).astype(F32).astype(BF)
    step = min(256, slots)
    for p in range(0, slots, step):
        ones = place_matrix(place, p, step)
        packed_out[p : p + step, :] = dot(ones, slots_scr[...]).astype(BF)
        code = dot_nt(parts, ones)
        table_out[:, p : p + step] = (code[0:1] * 32.0 + code[1:2]).astype(jnp.int32) - 1


def prep(count, cols, owner, pool, cot, groups, balance):
    slots = owner.shape[1]
    feature = cot.shape[1]
    return pl.pallas_call(
        functools.partial(prep_kernel, groups=groups, balance=balance),
        out_shape=(
            jax.ShapeDtypeStruct((1, slots), jnp.int32),
            jax.ShapeDtypeStruct((1, slots), jnp.int32),
            jax.ShapeDtypeStruct((slots, feature), BF),
        ),
        in_specs=[SM, SM, VM, VM, VM],
        out_specs=(VM, VM, VM),
        scratch_shapes=[pltpu.VMEM((slots, feature), BF)],
        compiler_params=params(),
        cost_estimate=cost(2 * slots * slots * 256, 4e6),
        name="prep_slots",
    )(count, cols, owner, pool, cot)


def layer_rows(x, message, w_in, w_out, bias):
    pre = dot(jnp.concatenate([x, message], axis=1), w_in) + bias
    hidden = (pre * jax.nn.sigmoid(pre)).astype(BF)
    return (x.astype(F32) + dot(hidden, w_out)).astype(BF)


def fine_inner_kernel(cols, feats, adj, w_in, w_out, bias, msg_out, res_out, *, rim):
    k = cols.shape[1]
    chunk = pl.program_id(0) + 1
    for j in range(CHUNK):
        block = apply_row(adj[j], cols, chunk * CHUNK + j, k, feats, rim)
        msg_out[j * BLK : (j + 1) * BLK, :] = block.astype(BF)
    rows = CHUNK * BLK
    x = feats[pl.ds(pl.multiple_of(chunk * rows, rows), rows), :]
    res_out[...] = layer_rows(x, msg_out[...], w_in[...], w_out[...], bias[...])


def fine_edge_kernel(cols, feats, prev, after, adj, w_in, w_out, bias, _m, _r, msg_out, res_out, ctx, *, rim):
    k = cols.shape[1]
    total = feats.shape[0]
    blocks = total // BLK
    rows = CHUNK * BLK
    width = rim * BLK
    upper = pl.program_id(0) == 1

    @pl.when(pl.program_id(0) == 0)
    def _():
        ctx[0:width, :] = prev[...]
        ctx[width:, :] = feats[0 : 2 * width, :]

    @pl.when(upper)
    def _():
        ctx[0 : 2 * width, :] = feats[total - 2 * width : total, :]
        ctx[2 * width :, :] = after[...]

    first = jnp.where(upper, blocks - CHUNK, 0)
    for j in range(CHUNK):
        block = apply_row(adj[j], cols, first + j, k, ctx, first)
        msg_out[j * BLK : (j + 1) * BLK, :] = block.astype(BF)
    x = feats[pl.ds(pl.multiple_of(first * BLK, rows), rows), :]
    res_out[...] = layer_rows(x, msg_out[...], w_in[...], w_out[...], bias[...])


def fine_forward(cols, feats, prev, after, adj, w_in, w_out, bias):
    total, feature = feats.shape
    blocks, _, span = adj.shape
    chunks = blocks // CHUNK
    rows = CHUNK * BLK
    rim = HALO // BLK
    out = (jax.ShapeDtypeStruct((total, feature), BF),) * 2
    inner_map = lambda c: (c + 1, 0)
    message, result = pl.pallas_call(
        functools.partial(fine_inner_kernel, rim=rim),
        grid=(chunks - 2,),
        out_shape=out,
        in_specs=[SM, VM, pl.BlockSpec((CHUNK, BLK, span), lambda c: (c + 1, 0, 0)), VM, VM, VM],
        out_specs=(pl.BlockSpec((rows, feature), inner_map),) * 2,
        compiler_params=params(),
        cost_estimate=cost(3e9, 2e7),
        name="fine_inner",
    )(cols, feats, adj, w_in, w_out, bias)
    edge_map = lambda c: (c * (chunks - 1), 0)
    return pl.pallas_call(
        functools.partial(fine_edge_kernel, rim=rim),
        grid=(2,),
        out_shape=out,
        in_specs=[
            SM,
            VM,
            VM,
            VM,
            pl.BlockSpec((CHUNK, BLK, span), lambda c: (c * (chunks - 1), 0, 0)),
            VM,
            VM,
            VM,
            pl.BlockSpec(memory_space=pl.ANY),
            pl.BlockSpec(memory_space=pl.ANY),
        ],
        out_specs=(pl.BlockSpec((rows, feature), edge_map),) * 2,
        scratch_shapes=[pltpu.VMEM((3 * HALO, feature), BF)],
        input_output_aliases={8: 0, 9: 1},
        compiler_params=params(),
        cost_estimate=cost(4e8, 4e6),
        name="fine_edge",
    )(cols, feats, prev, after, adj, w_in, w_out, bias, message, result)


def pool_kernel(cols, place, pool, src, packed_out, slots_scr):
    k = cols.shape[1]
    for q in range(pool.shape[0]):
        slots_scr[q * BLK : (q + 1) * BLK, :] = apply_row(pool[q], cols, q, k, src).astype(BF)
    slots = place.shape[1]
    step = min(256, slots)
    for p in range(0, slots, step):
        packed_out[p : p + step, :] = dot(place_matrix(place[...], p, step), slots_scr[...]).astype(BF)


def pool_pack(cols, place, pool, src):
    slots = place.shape[1]
    feature = src.shape[1]
    return pl.pallas_call(
        pool_kernel,
        out_shape=jax.ShapeDtypeStruct((slots, feature), BF),
        in_specs=[SM, VM, VM, VM],
        out_specs=VM,
        scratch_shapes=[pltpu.VMEM((slots, feature), BF)],
        compiler_params=params(),
        cost_estimate=cost(2 * slots * slots * 128, 3.5e6),
        name="pool_one_pack",
    )(cols, place, pool, src)


def place_kernel(table, got, own_out):
    own_out[...] = dot(place_matrix(table[...], 0, own_out.shape[0]), got[...]).astype(BF)


def place_rows(table, got, balance):
    return pl.pallas_call(
        place_kernel,
        out_shape=jax.ShapeDtypeStruct((balance, got.shape[1]), BF),
        in_specs=[VM, VM],
        out_specs=VM,
        compiler_params=params(),
        cost_estimate=cost(2 * balance * got.size, 1e6),
        name="place_own_one",
    )(table, got)


def place_pool_kernel(cols, count, table, got, pool, own_out, slots_out):
    k = cols.shape[1]
    own_out[...] = dot(place_matrix(table[...], 0, own_out.shape[0]), got[...]).astype(BF)
    for q in range(pool.shape[0]):
        slots_out[q * BLK : (q + 1) * BLK, :] = apply_row(pool[q], cols, q, k, own_out).astype(BF)


def place_pool(cols, count, table, got, pool, balance):
    feature = got.shape[1]
    return pl.pallas_call(
        place_pool_kernel,
        out_shape=(
            jax.ShapeDtypeStruct((balance, feature), BF),
            jax.ShapeDtypeStruct((pool.shape[0] * BLK, feature), BF),
        ),
        in_specs=[SM, SM, VM, VM, VM],
        out_specs=(VM, VM),
        compiler_params=params(),
        cost_estimate=cost(2 * balance * got.size, 1e6),
        name="place_grad_up_one",
    )(cols, count, table, got, pool)


def one_forward_kernel(cols, pool_cols, ctx, own, adj, pool, w_in, w_out, bias, msg_out, res_out, slots_out):
    k = cols.shape[1]
    for r in range(adj.shape[0]):
        msg_out[r * BLK : (r + 1) * BLK, :] = apply_row(adj[r], cols, r, k, ctx).astype(BF)
    res_out[...] = layer_rows(own[...], msg_out[...], w_in[...], w_out[...], bias[...])
    k = pool_cols.shape[1]
    for q in range(pool.shape[0]):
        slots_out[q * BLK : (q + 1) * BLK, :] = apply_row(pool[q], pool_cols, q, k, res_out).astype(BF)


def one_forward(cols, pool_cols, ctx, own, adj, pool, w_in, w_out, bias):
    own_shape = jax.ShapeDtypeStruct(own.shape, BF)
    return pl.pallas_call(
        one_forward_kernel,
        out_shape=(own_shape, own_shape, jax.ShapeDtypeStruct((pool.shape[0] * BLK, own.shape[1]), BF)),
        in_specs=[SM, SM] + [VM] * 7,
        out_specs=(VM, VM, VM),
        compiler_params=params(),
        cost_estimate=cost(2e8, 2.5e6),
        name="level_one_forward",
    )(cols, pool_cols, ctx, own, adj, pool, w_in, w_out, bias)


def grad_pre_rows(grad_low, x, message, w_in, w_out, bias):
    joined = jnp.concatenate([x, message], axis=1)
    pre = dot(joined, w_in) + bias
    sig = jax.nn.sigmoid(pre)
    hidden = (pre * sig).astype(BF)
    grad_pre = dot_nt(grad_low, w_out) * (sig * (1.0 + pre * (1.0 - sig)))
    return joined, hidden, grad_pre


def coarse_kernel(
    me, cols_two, cols_one, pool_cols, slots_two, gslots_two, own_two, mine_two, adj_two, adj_one, pool_two,
    table_one, own_one, msg_one, res_one, gup_one,
    wi1, wo1, b1, wi2, wo2, b2,
    upsend_out, gctx_out, gx_out, dwi1, dwo1, db1, dwi2, dwo2, db2,
    both, xs, gs, ms, hs, gps, rs, ctx_acc, up_acc, gmsg, gctx_acc,
):
    feature = own_one.shape[1]
    n2 = xs.shape[0]
    n1 = own_one.shape[0]
    both[:, :feature] = slots_two[...]
    both[:, feature:] = gslots_two[...]
    table = own_two[...]
    step = min(256, n2)
    for v in range(0, n2, step):
        rows = dot(place_matrix(table, v, step), both[...]).astype(BF)
        xs[v : v + step, :] = rows[:, :feature]
        gs[v : v + step, :] = rows[:, feature:]
    k = cols_two.shape[1]
    for r in range(adj_two.shape[0]):
        ms[r * BLK : (r + 1) * BLK, :] = apply_row(adj_two[r], cols_two, r, k, xs).astype(BF)
    ctx_acc[...] = jnp.zeros_like(ctx_acc)
    for v in range(0, n2, step):
        x, m, g = xs[v : v + step, :], ms[v : v + step, :], gs[v : v + step, :]
        joined, hidden, grad_pre = grad_pre_rows(g, x, m, wi2[...], wo2[...], b2[...])
        rs[v : v + step, :feature] = (x.astype(F32) + dot(hidden, wo2[...])).astype(BF)
        hs[v : v + step, :] = hidden
        gps[v : v + step, :] = grad_pre
        grad_joined = dot_nt(grad_pre.astype(BF), wi2[...])
        ctx_acc[v : v + step, :] += g.astype(F32) + grad_joined[:, :feature]
        gm = grad_joined[:, feature:].astype(BF)
        for j in range(step // BLK):
            r = v // BLK + j
            spread_row(adj_two[r], cols_two, r, k, gm[j * BLK : (j + 1) * BLK], ctx_acc)
    rs[:, feature:] = ctx_acc[...].astype(BF)
    balance = mine_two.shape[1] // 2
    at = pl.ds(pl.multiple_of(me[0] * balance, balance), balance)
    gp_own = gps[at, :]
    joined = jnp.concatenate([xs[at, :], ms[at, :]], axis=1)
    dwi2[...] = dot_tn(joined, gp_own.astype(BF))
    dwo2[...] = dot_tn(hs[at, :], gs[at, :])
    db2[...] = jnp.sum(gp_own, axis=0, keepdims=True)
    mine = place_matrix(mine_two[...], 0, n2)
    back = dot_tn(mine, rs[...]).astype(BF)
    up_acc[:, :feature] = res_one[...].astype(F32)
    up_acc[:, feature:] = gup_one[...].astype(F32)
    k = pool_cols.shape[1]
    for q in range(pool_two.shape[0]):
        spread_row(pool_two[q], pool_cols, q, k, back[q * BLK : (q + 1) * BLK], up_acc)
    ones = place_matrix(table_one[...], 0, n1)
    upsend_out[...] = dot_tn(ones, up_acc[:, :feature].astype(BF)).astype(BF)
    grad = up_acc[:, feature:]
    grad_low = grad.astype(BF)
    joined, hidden, grad_pre = grad_pre_rows(grad_low, own_one[...], msg_one[...], wi1[...], wo1[...], b1[...])
    grad_pre_low = grad_pre.astype(BF)
    dwi1[...] = dot_tn(joined, grad_pre_low)
    dwo1[...] = dot_tn(hidden, grad_low)
    db1[...] = jnp.sum(grad_pre, axis=0, keepdims=True)
    grad_joined = dot_nt(grad_pre_low, wi1[...])
    gx_out[...] = grad + grad_joined[:, :feature]
    gmsg[...] = grad_joined[:, feature:].astype(BF)
    gctx_acc[...] = jnp.zeros_like(gctx_acc)
    k = cols_one.shape[1]
    for r in range(adj_one.shape[0]):
        spread_row(adj_one[r], cols_one, r, k, gmsg[r * BLK : (r + 1) * BLK, :], gctx_acc)
    gctx_out[...] = gctx_acc[...].astype(BF)


def coarse_levels(
    me, cols_two, cols_one, pool_cols, slots_two, gslots_two, own_two, mine_two, adj_two, adj_one, pool_two,
    table_one, own_one, msg_one, res_one, gup_one, wi1, wo1, b1, wi2, wo2, b2, groups,
):
    n1, feature = own_one.shape
    n2 = adj_two.shape[0] * BLK
    slots_one = table_one.shape[1]
    weight_shapes = (
        jax.ShapeDtypeStruct((2 * feature, feature), F32),
        jax.ShapeDtypeStruct((feature, feature), F32),
        jax.ShapeDtypeStruct((1, feature), F32),
    )
    return pl.pallas_call(
        coarse_kernel,
        out_shape=(
            jax.ShapeDtypeStruct((slots_one, feature), BF),
            jax.ShapeDtypeStruct((groups * n1, feature), BF),
            jax.ShapeDtypeStruct((n1, feature), F32),
        )
        + weight_shapes * 2,
        in_specs=[SM] * 4 + [VM] * 18,
        out_specs=(VM,) * 9,
        scratch_shapes=[
            pltpu.VMEM((slots_two.shape[0], 2 * feature), BF),
            pltpu.VMEM((n2, feature), BF),
            pltpu.VMEM((n2, feature), BF),
            pltpu.VMEM((n2, feature), BF),
            pltpu.VMEM((n2, feature), BF),
            pltpu.VMEM((n2, feature), F32),
            pltpu.VMEM((n2, 2 * feature), BF),
            pltpu.VMEM((n2, feature), F32),
            pltpu.VMEM((n1, 2 * feature), F32),
            pltpu.VMEM((n1, feature), BF),
            pltpu.VMEM((groups * n1, feature), F32),
        ],
        compiler_params=params(),
        cost_estimate=cost(4e9, 8e6),
        name="coarse_levels",
    )(
        me, cols_two, cols_one, pool_cols, slots_two, gslots_two, own_two, mine_two, adj_two, adj_one, pool_two,
        table_one, own_one, msg_one, res_one, gup_one, wi1, wo1, b1, wi2, wo2, b2,
    )


def owner_sum_kernel(table, parts, gx, send_out):
    total = gx[...]
    for d in range(parts.shape[0]):
        total += parts[d].astype(F32)
    ones = place_matrix(table[...], 0, gx.shape[0])
    send_out[...] = dot_tn(ones, total.astype(BF)).astype(BF)


def owner_sum(table, parts, gx):
    return pl.pallas_call(
        owner_sum_kernel,
        out_shape=jax.ShapeDtypeStruct((table.shape[1], gx.shape[1]), BF),
        in_specs=[VM, VM, VM],
        out_specs=VM,
        compiler_params=params(),
        cost_estimate=cost(2 * table.shape[1] * gx.size, 2e6),
        name="grad_own_one_send",
    )(table, parts, gx)


def lift(place, got, pool, cols, acc):
    rows = dot_tn(place_matrix(place[...], 0, got.shape[0]), got[...]).astype(BF)
    k = cols.shape[1]
    for q in range(pool.shape[0]):
        spread_row(pool[q], cols, q, k, rows[q * BLK : (q + 1) * BLK], acc)


def node_out_kernel(cols, place, got, pool, base, out, acc):
    rows = out.shape[0]

    @pl.when(pl.program_id(0) == 0)
    def _():
        acc[...] = jnp.zeros_like(acc)
        lift(place, got, pool, cols, acc)

    at = pl.ds(pl.multiple_of(pl.program_id(0) * rows, rows), rows)
    out[...] = (base[...].astype(F32) + acc[at, :]).astype(BF)


def node_out_rows(cols, place, got, pool, base):
    total, feature = base.shape
    rows = 1024
    spec = pl.BlockSpec((rows, feature), lambda c: (c, 0))
    return pl.pallas_call(
        node_out_kernel,
        grid=(total // rows,),
        out_shape=jax.ShapeDtypeStruct((total, feature), BF),
        in_specs=[SM, VM, VM, VM, spec],
        out_specs=spec,
        scratch_shapes=[pltpu.VMEM((total, feature), F32)],
        compiler_params=params(),
        cost_estimate=cost(5e8, 6e6),
        name="node_out",
    )(cols, place, got, pool, base)


def fine_grad_kernel(
    cols, place, got, pool, cot, feats, message, w_in, w_out, bias, gx_out, gmsg_out, dwi, dwo, db, acc
):
    rows = cot.shape[0]
    feature = cot.shape[1]

    @pl.when(pl.program_id(0) == 0)
    def _():
        acc[...] = jnp.zeros_like(acc)
        dwi[...] = jnp.zeros_like(dwi)
        dwo[...] = jnp.zeros_like(dwo)
        db[...] = jnp.zeros_like(db)
        lift(place, got, pool, cols, acc)

    at = pl.ds(pl.multiple_of(pl.program_id(0) * rows, rows), rows)
    grad = cot[...].astype(F32) + acc[at, :]
    grad_low = grad.astype(BF)
    joined, hidden, grad_pre = grad_pre_rows(grad_low, feats[...], message[...], w_in[...], w_out[...], bias[...])
    grad_pre_low = grad_pre.astype(BF)
    dwi[...] += dot_tn(joined, grad_pre_low)
    dwo[...] += dot_tn(hidden, grad_low)
    db[...] += jnp.sum(grad_pre, axis=0, keepdims=True)
    grad_joined = dot_nt(grad_pre_low, w_in[...])
    gx_out[...] = grad + grad_joined[:, :feature]
    gmsg_out[...] = grad_joined[:, feature:].astype(BF)


def fine_grad(cols, place, got, pool, cot, feats, message, w_in, w_out, bias):
    total, feature = cot.shape
    rows = 512
    spec = pl.BlockSpec((rows, feature), lambda c: (c, 0))
    return pl.pallas_call(
        fine_grad_kernel,
        grid=(total // rows,),
        out_shape=(
            jax.ShapeDtypeStruct((total, feature), F32),
            jax.ShapeDtypeStruct((total, feature), BF),
            jax.ShapeDtypeStruct((2 * feature, feature), F32),
            jax.ShapeDtypeStruct((feature, feature), F32),
            jax.ShapeDtypeStruct((1, feature), F32),
        ),
        in_specs=[SM, VM, VM, VM, spec, spec, spec, VM, VM, VM],
        out_specs=(spec, spec, VM, VM, VM),
        scratch_shapes=[pltpu.VMEM((total, feature), F32)],
        compiler_params=params(),
        cost_estimate=cost(3e9, 1.5e7),
        name="fine_layer_backward",
    )(cols, place, got, pool, cot, feats, message, w_in, w_out, bias)


def fine_spread_kernel(cols, adj, gmsg, gx, mid_out, low_out, high_out, acc, *, rim):
    k = cols.shape[1]
    step = pl.program_id(0)
    steps = pl.num_programs(0)
    width = rim * BLK
    rows = CHUNK * BLK
    total = mid_out.shape[0]

    @pl.when(step == 0)
    def _():
        acc[...] = jnp.zeros_like(acc)

    for j in range(CHUNK):
        spread_row(adj[j], cols, step * CHUNK + j, k, gmsg[j * BLK : (j + 1) * BLK, :], acc)
    at = pl.ds(pl.multiple_of(width + step * rows, rows), rows)
    acc[at, :] += gx[...]

    @pl.when(step == steps - 1)
    def _():
        mid_out[...] = acc[width : width + total, :].astype(BF)
        low_out[0:width, :] = acc[0:width, :].astype(BF)
        low_out[width:, :] = acc[width + total :, :].astype(BF)
        high_out[0:width, :] = acc[width : 2 * width, :]
        high_out[width:, :] = acc[total : total + width, :]


def fine_spread(cols, adj, gmsg, gx):
    total, feature = gx.shape
    blocks, _, span = adj.shape
    rows = CHUNK * BLK
    spec = pl.BlockSpec((rows, feature), lambda c: (c, 0))
    return pl.pallas_call(
        functools.partial(fine_spread_kernel, rim=HALO // BLK),
        grid=(blocks // CHUNK,),
        out_shape=(
            jax.ShapeDtypeStruct((total, feature), BF),
            jax.ShapeDtypeStruct((2 * HALO, feature), BF),
            jax.ShapeDtypeStruct((2 * HALO, feature), F32),
        ),
        in_specs=[SM, pl.BlockSpec((CHUNK, BLK, span), lambda c: (c, 0, 0)), spec, spec],
        out_specs=(VM, VM, VM),
        scratch_shapes=[pltpu.VMEM((total + 2 * HALO, feature), F32)],
        compiler_params=params(),
        cost_estimate=cost(2e9, 2.2e7),
        name="fine_spread",
    )(cols, adj, gmsg, gx)


def rim_add_kernel(mid_in, rims, prev, after, out):
    got = jnp.where(pl.program_id(0) == 0, prev[...].astype(F32), after[...].astype(F32))
    out[...] = (rims[...] + got).astype(BF)


def rim_add(mid, rims, prev, after):
    total, feature = mid.shape
    return pl.pallas_call(
        rim_add_kernel,
        grid=(2,),
        out_shape=jax.ShapeDtypeStruct(mid.shape, BF),
        in_specs=[
            pl.BlockSpec(memory_space=pl.ANY),
            pl.BlockSpec((HALO, feature), lambda c: (c, 0)),
            VM,
            VM,
        ],
        out_specs=pl.BlockSpec((HALO, feature), lambda c: (c * (total // HALO - 1), 0)),
        input_output_aliases={0: 0},
        compiler_params=params(),
        cost_estimate=cost(1e6, 1.5e6),
        name="rim_add",
    )(mid, rims, prev, after)


def exchange(parts):
    return lax.all_to_all(parts, "grp", split_axis=0, concat_axis=0, tiled=True)


def gather_rows(rows):
    groups = lax.axis_size("grp")
    got = exchange(jnp.broadcast_to(rows[None], (groups,) + rows.shape))
    return got.reshape((groups * rows.shape[0],) + rows.shape[1:])


def halo_pair(low, high):
    count = lax.axis_size("grp")
    prev = lax.ppermute(high, "grp", [(i, i + 1) for i in range(count - 1)])
    after = lax.ppermute(low, "grp", [(i + 1, i) for i in range(count - 1)])
    return prev, after


def total_over_devices(rows):
    groups = lax.axis_size("grp")
    height = rows.shape[0]
    part = -(-height // (8 * groups)) * 8
    padded = jnp.pad(rows, ((0, part * groups - height), (0, 0)))
    mine = jnp.sum(exchange(padded.reshape(groups, part, rows.shape[1])), axis=0)
    slabs = lax.axis_size("slab")
    hop = 1
    while hop < slabs:
        mine = mine + lax.ppermute(mine, "slab", [(i, i ^ hop) for i in range(slabs)])
        hop *= 2
    return gather_rows(mine)[:height]


def body(
    node_feats,
    cotangent,
    fine_adjacency,
    fine_columns,
    pool_one,
    pool_one_columns,
    count_one,
    owner_one,
    adjacency_one,
    columns_one,
    pool_two,
    pool_two_columns,
    count_two,
    owner_two,
    adjacency_two,
    columns_two,
    weight_in,
    weight_out,
    biases,
):
    groups = lax.axis_size("grp")
    feature = node_feats.shape[1]
    slots_one = owner_one.shape[0]
    balance_one = slots_one // 2
    slots_two = owner_two.shape[0]
    me = lax.axis_index("grp").astype(jnp.int32).reshape(1)
    bias_rows = [biases[level : level + 1] for level in range(3)]

    prev, after = halo_pair(node_feats[:HALO], node_feats[-HALO:])
    adjacency_two_all = lax.all_gather(adjacency_two, "grp", axis=0, tiled=True)
    place_one, table_sent, gslots_send = prep(
        count_one, pool_one_columns, owner_one.reshape(1, slots_one), pool_one, cotangent, groups, balance_one
    )
    mine_two = jnp.where(jnp.arange(slots_two) < count_two[0], owner_two, -1).astype(jnp.int32)
    ints_two = jnp.concatenate([mine_two, columns_two.reshape(-1)])
    ints = exchange(
        jnp.concatenate(
            [table_sent.reshape(groups, -1), jnp.broadcast_to(ints_two[None], (groups, ints_two.shape[0]))], axis=1
        )[:, None, :]
    )[:, 0, :]
    cap_one = slots_one // groups
    table_one = ints[:, :cap_one].reshape(1, slots_one)
    own_two_all = ints[:, cap_one : cap_one + slots_two].reshape(1, groups * slots_two)
    columns_two_all = ints[:, cap_one + slots_two :].reshape(-1, columns_two.shape[1])
    gslots_got = exchange(gslots_send.reshape(groups, cap_one, feature))

    message0, result0 = fine_forward(
        fine_columns, node_feats, prev, after, fine_adjacency, weight_in[0], weight_out[0], bias_rows[0]
    )
    sent_one = pool_pack(pool_one_columns, place_one, pool_one, result0)
    got_one = exchange(sent_one.reshape(groups, cap_one, feature))
    own_one = place_rows(table_one, got_one.reshape(slots_one, feature), balance_one)
    context_one = gather_rows(own_one)

    grad_up_one, gslots_two = place_pool(
        pool_two_columns, count_two, table_one, gslots_got.reshape(slots_one, feature), pool_two, balance_one
    )
    gslots_two_all = gather_rows(gslots_two)

    message_one, result1, coarse_two = one_forward(
        columns_one, pool_two_columns, context_one, own_one, adjacency_one, pool_two,
        weight_in[1], weight_out[1], bias_rows[1],
    )
    coarse_two_all = gather_rows(coarse_two)

    up_send, gctx_one, gx_one, dwi1, dwo1, db1, dwi2, dwo2, db2 = coarse_levels(
        me, columns_two_all, columns_one, pool_two_columns, coarse_two_all, gslots_two_all, own_two_all,
        mine_two.reshape(1, slots_two), adjacency_two_all, adjacency_one, pool_two,
        table_one, own_one, message_one, result1, grad_up_one,
        weight_in[1], weight_out[1], bias_rows[1], weight_in[2], weight_out[2], bias_rows[2], groups,
    )
    gctx_parts = exchange(gctx_one.reshape(groups, balance_one, feature))
    up_got = exchange(up_send.reshape(groups, cap_one, feature)).reshape(slots_one, feature)
    grad_send = owner_sum(table_one, gctx_parts, gx_one)
    grad_got = exchange(grad_send.reshape(groups, cap_one, feature)).reshape(slots_one, feature)
    node_out = node_out_rows(pool_one_columns, place_one, up_got, pool_one, result0)

    coarse_sums = total_over_devices(jnp.concatenate([dwi1, dwo1, dwi2, dwo2, db1, db2], axis=0))

    gx_zero, gmsg_zero, dwi0, dwo0, db0 = fine_grad(
        pool_one_columns, place_one, grad_got, pool_one, cotangent, node_feats, message0,
        weight_in[0], weight_out[0], bias_rows[0],
    )
    fine_sums = total_over_devices(jnp.concatenate([dwi0, dwo0, db0], axis=0))
    mid, rims_out, rims_own = fine_spread(fine_columns, fine_adjacency, gmsg_zero, gx_zero)
    from_prev, from_after = halo_pair(rims_out[:HALO], rims_out[HALO:])
    grad_feats = rim_add(mid, rims_own, from_prev, from_after)

    scale = 1.0 / math.sqrt(node_feats.shape[0] * groups * lax.axis_size("slab"))
    wide = 2 * feature
    level = wide + feature
    grad_in = jnp.stack([fine_sums[:wide], coarse_sums[:wide], coarse_sums[level : level + wide]])
    grad_out = jnp.stack([fine_sums[wide:level], coarse_sums[wide:level], coarse_sums[level + wide : 2 * level]])
    grad_bias = jnp.concatenate([fine_sums[level : level + 1], coarse_sums[2 * level : 2 * level + 2]])
    return (node_out, grad_feats, grad_in * scale, grad_out * scale, grad_bias * scale)


def solution(mesh):
    rows = P(("slab", "grp"), None)
    blocks = P(("slab", "grp"), None, None)
    flat = P(("slab", "grp"))
    placed = (
        rows, rows, blocks, rows, blocks, rows, flat, flat, blocks, rows,
        blocks, rows, flat, flat, blocks, rows, P(), P(), P(),
    )
    return jax.shard_map(
        body,
        mesh=mesh,
        in_specs=placed,
        out_specs=(rows, rows, P(), P(), P()),
        check_vma=False,
    )
```

```python
import functools
import math

import jax
import jax.numpy as jnp
from jax import lax
from jax.experimental import pallas as pl
from jax.experimental.pallas import tpu as pltpu
from jax.sharding import PartitionSpec as P

BF = jnp.bfloat16
F32 = jnp.float32
HALO = 512
BLK = 64
CHUNK = 8
EXTRA = 16
VMEM_LIMIT = 56 * 1024 * 1024

VM = pl.BlockSpec(memory_space=pltpu.VMEM)
SM = pl.BlockSpec(memory_space=pltpu.SMEM)


def params():
    return pltpu.CompilerParams(vmem_limit_bytes=VMEM_LIMIT)


def takes(microseconds):
    return pl.CostEstimate(flops=0, bytes_accessed=int(3 * microseconds * 3.69e6), transcendentals=0)


def dot(a, b):
    return jnp.dot(a, b, preferred_element_type=F32)


def dot_nt(a, b):
    return lax.dot_general(a, b, (((1,), (1,)), ((), ())), preferred_element_type=F32)


def dot_tn(a, b):
    return lax.dot_general(a, b, (((0,), (0,)), ((), ())), preferred_element_type=F32)


def iota(shape, dim):
    return lax.broadcasted_iota(jnp.int32, shape, dim)


def as_ones(mask):
    return jnp.where(mask, 1.0, 0.0).astype(BF)


def tile_at(ref, index):
    return ref[pl.ds(pl.multiple_of(index * BLK, BLK), BLK), :]


def apply_row(block, cols, r, count, ref, shift=0):
    picked = jnp.concatenate([tile_at(ref, cols[r, i] - shift) for i in range(count)], axis=0)
    return dot(block, picked)


def spread_row(block, cols, r, count, rows, acc, shift=0):
    spread = dot_tn(block, rows)
    for i in range(count):
        at = pl.ds(pl.multiple_of((cols[r, i] - shift) * BLK, BLK), BLK)
        acc[at, :] += spread[i * BLK : (i + 1) * BLK]


def place_matrix(row_table, first, count):
    n = row_table.shape[1]
    return as_ones(row_table == iota((count, n), 0) + first)


def digits(values):
    shifted = values + 1
    return (shifted >> 6).astype(F32), (shifted & 63).astype(F32)


def from_digits(high, low):
    return (high.astype(F32) * 64.0 + low.astype(F32)).astype(jnp.int32) - 1


def lane_rows(values):
    n = values.shape[1]
    rows = []
    for at in range(0, n, 128):
        row = values[:, at : min(at + 128, n)]
        if row.shape[1] < 128:
            row = jnp.concatenate([row, jnp.zeros((1, 128 - row.shape[1]), F32)], axis=1)
        rows.append(row)
    return rows


def prep_kernel(
    count, cols, count_two, owner_ref, two_ref, cols_two, pool, cot, adj_two, place_out, mine_out, send_out, slots_scr,
    *, groups, balance,
):
    slots = owner_ref.shape[1]
    cap = slots // groups
    k = cols.shape[1]
    for q in range(pool.shape[0]):
        slots_scr[q * BLK : (q + 1) * BLK, :] = apply_row(pool[q], cols, q, k, cot).astype(BF)
    owner = owner_ref[...]
    live = iota((1, slots), 1) < count[0]
    rows = max(16, groups)
    target = iota((rows, slots), 0)
    low = target * balance
    hit = (owner >= low) & (owner < low + balance) & live
    onehot = jnp.where(hit, 1.0, 0.0)
    upper = as_ones(iota((slots, slots), 0) <= iota((slots, slots), 1))
    running = dot(onehot.astype(BF), upper)
    rank = jnp.sum(onehot * running, axis=0, keepdims=True) - 1.0
    base = jnp.sum(jnp.where(hit, target * cap, 0).astype(F32), axis=0, keepdims=True)
    start = jnp.sum(jnp.where(hit, low, 0).astype(F32), axis=0, keepdims=True)
    place = jnp.where(live, (base + rank).astype(jnp.int32), slots)
    place_out[...] = place
    two = two_ref[...]
    two = jnp.where(iota(two.shape, 1) < count_two[0], two, -1)
    mine_out[...] = two
    two_high, two_low = digits(two)
    shared = lane_rows(two_high) + lane_rows(two_low) + lane_rows(cols_two[...].astype(F32))
    local_high, local_low = digits(owner - start.astype(jnp.int32))
    kind = iota((rows, slots), 0)
    parts = jnp.where(kind == 0, local_high, jnp.where(kind == 1, local_low, 0.0)).astype(BF)
    for d in range(groups):
        ones = place_matrix(place, d * cap, cap)
        send_out[d, 0:cap, :] = dot(ones, slots_scr[...]).astype(BF)
        code = dot_nt(parts, ones)
        if cap < 128:
            code = jnp.concatenate([code, jnp.zeros((rows, 128 - cap), F32)], axis=1)
        tail = [code[0:1], code[1:2]] + shared
        tail = jnp.concatenate(tail + [jnp.zeros((EXTRA - len(tail), 128), F32)], axis=0)
        send_out[d, cap : cap + EXTRA, :] = tail.astype(BF)
        at = cap + EXTRA
        for r in range(adj_two.shape[0]):
            for c in range(0, adj_two.shape[2], 128):
                send_out[d, at : at + BLK, :] = adj_two[r, :, c : c + 128]
                at += BLK


def prep(count, cols, count_two, owner, two, cols_two, pool, cot, adj_two, groups, balance):
    slots = owner.shape[1]
    feature = cot.shape[1]
    height = slots // groups + EXTRA + adj_two.size // 128
    return pl.pallas_call(
        functools.partial(prep_kernel, groups=groups, balance=balance),
        out_shape=(
            jax.ShapeDtypeStruct((1, slots), jnp.int32),
            jax.ShapeDtypeStruct(two.shape, jnp.int32),
            jax.ShapeDtypeStruct((groups, height, feature), BF),
        ),
        in_specs=[SM, SM, SM, VM, VM, VM, VM, VM, VM],
        out_specs=(VM, VM, VM),
        scratch_shapes=[pltpu.VMEM((slots, feature), BF)],
        compiler_params=params(),
        cost_estimate=takes(5),
        name="prep_slots",
    )(count, cols, count_two, owner, two, cols_two, pool, cot, adj_two)


def layer_rows(x, message, w_in, w_out, bias):
    pre = dot(jnp.concatenate([x, message], axis=1), w_in) + bias
    hidden = (pre * jax.nn.sigmoid(pre)).astype(BF)
    return (x.astype(F32) + dot(hidden, w_out)).astype(BF)


def fine_inner_kernel(cols, feats_hbm, adj_hbm, w_in, w_out, bias, *refs, rim, first, last):
    msg_out, res_out, feats, adj, feats_sem, adj_sem = refs[-6:]
    k = cols.shape[1]
    step = pl.program_id(0)
    chunk = step + first
    rows = CHUNK * BLK

    def feats_copy(c):
        at = pl.ds(pl.multiple_of(c * rows, rows), rows)
        return pltpu.make_async_copy(feats_hbm.at[at, :], feats.at[at, :], feats_sem.at[c - first + 1])

    def adj_copy(c):
        source = adj_hbm.at[pl.ds(c * CHUNK, CHUNK)]
        return pltpu.make_async_copy(source, adj.at[pl.ds((c - first) * CHUNK, CHUNK)], adj_sem.at[c - first])

    @pl.when(step == 0)
    def _():
        for c in (first - 1, first, first + 1):
            feats_copy(c).start()
        for c in range(first, last):
            adj_copy(c).start()
            if c + 2 <= last:
                feats_copy(c + 2).start()
        feats_copy(first - 1).wait()
        feats_copy(first).wait()

    feats_copy(chunk + 1).wait()
    adj_copy(chunk).wait()
    for j in range(CHUNK):
        block = apply_row(adj[step * CHUNK + j], cols, chunk * CHUNK + j, k, feats, rim)
        msg_out[j * BLK : (j + 1) * BLK, :] = block.astype(BF)
    x = feats[pl.ds(pl.multiple_of(chunk * rows, rows), rows), :]
    res_out[...] = layer_rows(x, msg_out[...], w_in[...], w_out[...], bias[...])


def fine_inner(cols, feats, adj, w_in, w_out, bias, first, last, done):
    total, feature = feats.shape
    rows = CHUNK * BLK
    steps = last - first
    hbm = pl.BlockSpec(memory_space=pl.ANY)
    return pl.pallas_call(
        functools.partial(fine_inner_kernel, rim=HALO // BLK, first=first, last=last),
        grid=(steps,),
        out_shape=(jax.ShapeDtypeStruct((total, feature), BF),) * 2,
        in_specs=[SM, hbm, hbm, VM, VM, VM] + [hbm] * len(done),
        out_specs=(pl.BlockSpec((rows, feature), lambda c: (c + first, 0)),) * 2,
        scratch_shapes=[
            pltpu.VMEM((total, feature), BF),
            pltpu.VMEM((steps * CHUNK,) + adj.shape[1:], BF),
            pltpu.SemaphoreType.DMA((steps + 2,)),
            pltpu.SemaphoreType.DMA((steps,)),
        ],
        input_output_aliases={6 + i: i for i in range(len(done))},
        compiler_params=params(),
        cost_estimate=takes(1.1 * steps),
        name="fine_inner",
    )(cols, feats, adj, w_in, w_out, bias, *done)


def fine_edge_kernel(me, cols, feats, prev, after, adj, w_in, w_out, bias, _m, _r, msg_out, res_out, ctx, *, blocks, groups):
    k = cols.shape[1]
    rows = CHUNK * BLK
    width = prev.shape[0]
    upper = pl.program_id(0) == 1

    @pl.when(pl.program_id(0) == 0)
    def _():
        ctx[0:width, :] = jnp.where(me[0] > 0, prev[...], jnp.zeros_like(prev))
        ctx[width:, :] = feats[...]

    @pl.when(upper)
    def _():
        ctx[0 : 2 * width, :] = feats[...]
        ctx[2 * width :, :] = jnp.where(me[0] < groups - 1, after[...], jnp.zeros_like(after))

    first = jnp.where(upper, blocks - CHUNK, 0)
    for j in range(CHUNK):
        block = apply_row(adj[j], cols, first + j, k, ctx, first)
        msg_out[j * BLK : (j + 1) * BLK, :] = block.astype(BF)
    x = ctx[width : width + rows, :]
    res_out[...] = layer_rows(x, msg_out[...], w_in[...], w_out[...], bias[...])


def fine_edge(me, groups, cols, feats, prev, after, adj, w_in, w_out, bias, message, result):
    total, feature = feats.shape
    blocks, _, span = adj.shape
    chunks = blocks // CHUNK
    rows = CHUNK * BLK
    out = (jax.ShapeDtypeStruct((total, feature), BF),) * 2
    edge_map = lambda c: (c * (chunks - 1), 0)
    return pl.pallas_call(
        functools.partial(fine_edge_kernel, blocks=blocks, groups=groups),
        grid=(2,),
        out_shape=out,
        in_specs=[
            SM,
            SM,
            pl.BlockSpec((2 * HALO, feature), lambda c: (c * (total // (2 * HALO) - 1), 0)),
            VM,
            VM,
            pl.BlockSpec((CHUNK, BLK, span), lambda c: (c * (chunks - 1), 0, 0)),
            VM,
            VM,
            VM,
            pl.BlockSpec(memory_space=pl.ANY),
            pl.BlockSpec(memory_space=pl.ANY),
        ],
        out_specs=(pl.BlockSpec((rows, feature), edge_map),) * 2,
        scratch_shapes=[pltpu.VMEM((3 * HALO, feature), BF)],
        input_output_aliases={9: 0, 10: 1},
        compiler_params=params(),
        cost_estimate=takes(4),
        name="fine_edge",
    )(me, cols, feats, prev, after, adj, w_in, w_out, bias, message, result)


def pool_kernel(cols, place, pool, src, packed_out, slots_scr):
    k = cols.shape[1]
    for q in range(pool.shape[0]):
        slots_scr[q * BLK : (q + 1) * BLK, :] = apply_row(pool[q], cols, q, k, src).astype(BF)
    slots = place.shape[1]
    step = min(256, slots)
    for p in range(0, slots, step):
        packed_out[p : p + step, :] = dot(place_matrix(place[...], p, step), slots_scr[...]).astype(BF)


def pool_pack(cols, place, pool, src):
    slots = place.shape[1]
    feature = src.shape[1]
    return pl.pallas_call(
        pool_kernel,
        out_shape=jax.ShapeDtypeStruct((slots, feature), BF),
        in_specs=[SM, VM, VM, VM],
        out_specs=VM,
        scratch_shapes=[pltpu.VMEM((slots, feature), BF)],
        compiler_params=params(),
        cost_estimate=takes(4),
        name="pool_one_pack",
    )(cols, place, pool, src)


def place_all(tables, got, n, cap):
    own = jnp.zeros((n, got.shape[2]), F32)
    for d in range(got.shape[0]):
        own += dot(place_matrix(tables[d], 0, n), got[d, 0:cap, :])
    return own.astype(BF)


def tables_from(first, cap):
    return [
        from_digits(first[d, cap : cap + 1, :], first[d, cap + 1 : cap + 2, :])[:, :cap]
        for d in range(first.shape[0])
    ]


def place_kernel(first, got, own_out):
    cap = got.shape[1]
    own_out[...] = place_all(tables_from(first, cap), got, own_out.shape[0], cap)


def place_rows(first, got, balance):
    groups, cap, feature = got.shape
    return pl.pallas_call(
        place_kernel,
        grid=(1,),
        out_shape=jax.ShapeDtypeStruct((balance, feature), BF),
        in_specs=[pl.BlockSpec((groups, cap + EXTRA, feature), lambda c: (0, 0, 0)), VM],
        out_specs=VM,
        compiler_params=params(),
        cost_estimate=takes(3),
        name="place_own_one",
    )(first, got)


def place_pool_kernel(cols, first, pool, own_out, slots_out, table_out):
    k = cols.shape[1]
    cap = table_out.shape[1]
    tables = tables_from(first, cap)
    own_out[...] = place_all(tables, first, own_out.shape[0], cap)
    for d in range(first.shape[0]):
        table_out[d : d + 1, :] = tables[d]
    for q in range(pool.shape[0]):
        slots_out[q * BLK : (q + 1) * BLK, :] = apply_row(pool[q], cols, q, k, own_out).astype(BF)


def place_pool(cols, first, pool, balance, cap):
    groups, _, feature = first.shape
    return pl.pallas_call(
        place_pool_kernel,
        grid=(1,),
        out_shape=(
            jax.ShapeDtypeStruct((balance, feature), BF),
            jax.ShapeDtypeStruct((pool.shape[0] * BLK, feature), BF),
            jax.ShapeDtypeStruct((groups, cap), jnp.int32),
        ),
        in_specs=[SM, pl.BlockSpec((groups, cap + EXTRA, feature), lambda c: (0, 0, 0)), VM],
        out_specs=(VM, VM, VM),
        compiler_params=params(),
        cost_estimate=takes(3),
        name="place_grad_up_one",
    )(cols, first, pool)


def one_forward_kernel(me, cols, pool_cols, *refs):
    pieces = refs[:-10]
    gslots, adj, pool, w_in, w_out, bias, msg_out, res_out, slots_out, ctx = refs[-10:]
    own = pieces[0]
    n = own.shape[0]
    for hop, piece in enumerate(pieces):
        ctx[pl.ds(pl.multiple_of((me[0] ^ hop) * n, n), n), :] = piece[...]
    k = cols.shape[1]
    for r in range(adj.shape[0]):
        msg_out[r * BLK : (r + 1) * BLK, :] = apply_row(adj[r], cols, r, k, ctx).astype(BF)
    res_out[...] = layer_rows(own[...], msg_out[...], w_in[...], w_out[...], bias[...])
    k = pool_cols.shape[1]
    for q in range(pool.shape[0]):
        rows = apply_row(pool[q], pool_cols, q, k, res_out).astype(BF)
        slots_out[q * BLK : (q + 1) * BLK, 0 : rows.shape[1]] = rows
    slots_out[:, own.shape[1] :] = gslots[...]


def one_forward(me, cols, pool_cols, pieces, gslots, adj, pool, w_in, w_out, bias):
    own = pieces[0]
    own_shape = jax.ShapeDtypeStruct(own.shape, BF)
    return pl.pallas_call(
        one_forward_kernel,
        out_shape=(own_shape, own_shape, jax.ShapeDtypeStruct((pool.shape[0] * BLK, 2 * own.shape[1]), BF)),
        in_specs=[SM, SM, SM] + [VM] * (len(pieces) + 6),
        out_specs=(VM, VM, VM),
        scratch_shapes=[pltpu.VMEM((len(pieces) * own.shape[0], own.shape[1]), BF)],
        compiler_params=params(),
        cost_estimate=takes(3),
        name="level_one_forward",
    )(me, cols, pool_cols, *pieces, gslots, adj, pool, w_in, w_out, bias)


def grad_pre_rows(grad_low, x, message, w_in, w_out, bias):
    joined = jnp.concatenate([x, message], axis=1)
    pre = dot(joined, w_in) + bias
    sig = jax.nn.sigmoid(pre)
    hidden = (pre * sig).astype(BF)
    grad_pre = dot_nt(grad_low, w_out) * (sig * (1.0 + pre * (1.0 - sig)))
    return joined, hidden, grad_pre


def coarse_kernel(groups, me, cols_two, cols_one, pool_cols, *refs):
    slots_two, refs = refs[:groups], refs[groups:]
    (
        mine_two, first, adj_one, pool_two, table_one, own_one, msg_one, res_one, gup_one,
        wi1, wo1, b1, wi2, wo2, b2, up_out, gx_out, sums_out,
    ) = refs[:18]
    part_outs, refs = refs[18 : 18 + groups - 1], refs[18 + groups - 1 :]
    both, xs, gs, ms, hs, gps, rs, ctx_acc, up_acc, gmsg, gctx_acc = refs
    feature = own_one.shape[1]
    n2 = xs.shape[0]
    n1 = own_one.shape[0]
    slots = mine_two.shape[1]
    for hop in range(groups):
        both[pl.ds(pl.multiple_of((me[0] ^ hop) * slots, slots), slots), :] = slots_two[hop][...]
    cap = table_one.shape[1]
    lanes = slots // 128
    at = cap + 2
    table = jnp.concatenate(
        [
            from_digits(first[d, at + c : at + c + 1, :], first[d, at + lanes + c : at + lanes + c + 1, :])
            for d in range(first.shape[0])
            for c in range(lanes)
        ],
        axis=1,
    )
    step = min(256, n2)
    for v in range(0, n2, step):
        rows = dot(place_matrix(table, v, step), both[...]).astype(BF)
        xs[v : v + step, :] = rows[:, :feature]
        gs[v : v + step, :] = rows[:, feature:]
    k = cols_two.shape[1]
    wide = k * BLK // 128

    def adj(r):
        per = n2 // (BLK * groups)
        at = cap + EXTRA + (r % per) * wide * BLK
        return jnp.concatenate(
            [first[r // per, at + c * BLK : at + (c + 1) * BLK, :] for c in range(wide)], axis=1
        )

    for r in range(n2 // BLK):
        ms[r * BLK : (r + 1) * BLK, :] = apply_row(adj(r), cols_two, r, k, xs).astype(BF)
    ctx_acc[...] = jnp.zeros_like(ctx_acc)
    for v in range(0, n2, step):
        x, m, g = xs[v : v + step, :], ms[v : v + step, :], gs[v : v + step, :]
        joined, hidden, grad_pre = grad_pre_rows(g, x, m, wi2[...], wo2[...], b2[...])
        rs[v : v + step, :feature] = (x.astype(F32) + dot(hidden, wo2[...])).astype(BF)
        hs[v : v + step, :] = hidden
        gps[v : v + step, :] = grad_pre
        grad_joined = dot_nt(grad_pre.astype(BF), wi2[...])
        ctx_acc[v : v + step, :] += g.astype(F32) + grad_joined[:, :feature]
        gm = grad_joined[:, feature:].astype(BF)
        for j in range(step // BLK):
            r = v // BLK + j
            spread_row(adj(r), cols_two, r, k, gm[j * BLK : (j + 1) * BLK], ctx_acc)
    rs[:, feature:] = ctx_acc[...].astype(BF)
    balance = slots // 2
    at = pl.ds(pl.multiple_of(me[0] * balance, balance), balance)
    gp_own = gps[at, :]
    joined = jnp.concatenate([xs[at, :], ms[at, :]], axis=1)
    level = 3 * feature
    sums_out[level : level + 2 * feature, :] = dot_tn(joined, gp_own.astype(BF))
    sums_out[level + 2 * feature : 2 * level, :] = dot_tn(hs[at, :], gs[at, :])
    bias_two = jnp.sum(gp_own, axis=0, keepdims=True)
    mine = place_matrix(mine_two[...], 0, n2)
    back = dot_tn(mine, rs[...]).astype(BF)
    up_acc[:, :feature] = res_one[...].astype(F32)
    up_acc[:, feature:] = gup_one[...].astype(F32)
    k = pool_cols.shape[1]
    for q in range(pool_two.shape[0]):
        spread_row(pool_two[q], pool_cols, q, k, back[q * BLK : (q + 1) * BLK], up_acc)
    up_low = up_acc[:, :feature].astype(BF)
    for d in range(table_one.shape[0]):
        up_out[d] = dot_tn(place_matrix(table_one[d : d + 1, :], 0, n1), up_low).astype(BF)
    grad = up_acc[:, feature:]
    grad_low = grad.astype(BF)
    joined, hidden, grad_pre = grad_pre_rows(grad_low, own_one[...], msg_one[...], wi1[...], wo1[...], b1[...])
    grad_pre_low = grad_pre.astype(BF)
    sums_out[0 : 2 * feature, :] = dot_tn(joined, grad_pre_low)
    sums_out[2 * feature : level, :] = dot_tn(hidden, grad_low)
    bias_one = jnp.sum(grad_pre, axis=0, keepdims=True)
    rest = sums_out.shape[0] - 2 * level
    row = iota((rest, feature), 0)
    sums_out[2 * level :, :] = jnp.where(row == 0, bias_one, jnp.where(row == 1, bias_two, 0.0))
    grad_joined = dot_nt(grad_pre_low, wi1[...])
    gmsg[...] = grad_joined[:, feature:].astype(BF)
    gctx_acc[...] = jnp.zeros_like(gctx_acc)
    k = cols_one.shape[1]
    for r in range(adj_one.shape[0]):
        spread_row(adj_one[r], cols_one, r, k, gmsg[r * BLK : (r + 1) * BLK, :], gctx_acc)
    own_at = pl.ds(pl.multiple_of(me[0] * n1, n1), n1)
    gx_out[...] = grad + grad_joined[:, :feature] + gctx_acc[own_at, :]
    for hop in range(1, groups):
        at = pl.ds(pl.multiple_of((me[0] ^ hop) * n1, n1), n1)
        part_outs[hop - 1][...] = gctx_acc[at, :].astype(BF)


def coarse_levels(
    me, cols_two, cols_one, pool_cols, slots_two, mine_two, first, adj_one, pool_two,
    table_one, own_one, msg_one, res_one, gup_one, wi1, wo1, b1, wi2, wo2, b2, sum_rows,
):
    groups = len(slots_two)
    n1, feature = own_one.shape
    n2 = mine_two.shape[1] // 2 * groups
    cap = table_one.shape[1]
    return pl.pallas_call(
        functools.partial(coarse_kernel, groups),
        out_shape=(
            jax.ShapeDtypeStruct((groups, cap, feature), BF),
            jax.ShapeDtypeStruct((n1, feature), F32),
            jax.ShapeDtypeStruct((sum_rows, feature), F32),
        )
        + (jax.ShapeDtypeStruct((n1, feature), BF),) * (groups - 1),
        in_specs=[SM] * 4 + [VM] * (15 + groups),
        out_specs=(VM,) * (2 + groups),
        scratch_shapes=[
            pltpu.VMEM((groups * slots_two[0].shape[0], 2 * feature), BF),
            pltpu.VMEM((n2, feature), BF),
            pltpu.VMEM((n2, feature), BF),
            pltpu.VMEM((n2, feature), BF),
            pltpu.VMEM((n2, feature), BF),
            pltpu.VMEM((n2, feature), F32),
            pltpu.VMEM((n2, 2 * feature), BF),
            pltpu.VMEM((n2, feature), F32),
            pltpu.VMEM((n1, 2 * feature), F32),
            pltpu.VMEM((n1, feature), BF),
            pltpu.VMEM((groups * n1, feature), F32),
        ],
        compiler_params=params(),
        cost_estimate=takes(9),
        name="coarse_levels",
    )(
        me, cols_two, cols_one, pool_cols, *slots_two, mine_two, first, adj_one, pool_two,
        table_one, own_one, msg_one, res_one, gup_one, wi1, wo1, b1, wi2, wo2, b2,
    )


def owner_sum_kernel(table, gx, *refs):
    send_out = refs[-1]
    total = gx[...]
    for part in refs[:-1]:
        total += part[...].astype(F32)
    low = total.astype(BF)
    for d in range(table.shape[0]):
        send_out[d] = dot_tn(place_matrix(table[d : d + 1, :], 0, gx.shape[0]), low).astype(BF)


def owner_sum(table, gx, parts):
    return pl.pallas_call(
        owner_sum_kernel,
        out_shape=jax.ShapeDtypeStruct(table.shape + (gx.shape[1],), BF),
        in_specs=[VM] * (2 + len(parts)),
        out_specs=VM,
        compiler_params=params(),
        cost_estimate=takes(3),
        name="grad_own_one_send",
    )(table, gx, *parts)


def lift(place, got, pool, cols, acc):
    groups, height, _ = got.shape
    cap = place.shape[1] // groups
    packed = jnp.concatenate([got[d, height - cap :, :] for d in range(groups)], axis=0)
    rows = dot_tn(place_matrix(place[...], 0, packed.shape[0]), packed).astype(BF)
    k = cols.shape[1]
    for q in range(pool.shape[0]):
        spread_row(pool[q], cols, q, k, rows[q * BLK : (q + 1) * BLK], acc)


def node_out_kernel(cols, place, got, pool, base, out, acc):
    rows = out.shape[0]

    @pl.when(pl.program_id(0) == 0)
    def _():
        acc[...] = jnp.zeros_like(acc)
        lift(place, got, pool, cols, acc)

    at = pl.ds(pl.multiple_of(pl.program_id(0) * rows, rows), rows)
    out[...] = (base[...].astype(F32) + acc[at, :]).astype(BF)


def node_out_rows(cols, place, got, pool, base):
    total, feature = base.shape
    rows = 1024
    spec = pl.BlockSpec((rows, feature), lambda c: (c, 0))
    return pl.pallas_call(
        node_out_kernel,
        grid=(total // rows,),
        out_shape=jax.ShapeDtypeStruct((total, feature), BF),
        in_specs=[SM, VM, VM, VM, spec],
        out_specs=spec,
        scratch_shapes=[pltpu.VMEM((total, feature), F32)],
        compiler_params=params(),
        cost_estimate=takes(9),
        name="node_out",
    )(cols, place, got, pool, base)


def fine_grad_kernel(
    cols, place, got, pool, cot, feats, message, w_in, w_out, bias, gx_out, gmsg_out, sums, acc
):
    rows = cot.shape[0]
    feature = cot.shape[1]

    @pl.when(pl.program_id(0) == 0)
    def _():
        acc[...] = jnp.zeros_like(acc)
        sums[...] = jnp.zeros_like(sums)
        lift(place, got, pool, cols, acc)

    at = pl.ds(pl.multiple_of(pl.program_id(0) * rows, rows), rows)
    grad = cot[...].astype(F32) + acc[at, :]
    grad_low = grad.astype(BF)
    joined, hidden, grad_pre = grad_pre_rows(grad_low, feats[...], message[...], w_in[...], w_out[...], bias[...])
    grad_pre_low = grad_pre.astype(BF)
    level = 3 * feature
    sums[0 : 2 * feature, :] += dot_tn(joined, grad_pre_low)
    sums[2 * feature : level, :] += dot_tn(hidden, grad_low)
    sums[level : level + 1, :] += jnp.sum(grad_pre, axis=0, keepdims=True)
    grad_joined = dot_nt(grad_pre_low, w_in[...])
    gx_out[...] = grad + grad_joined[:, :feature]
    gmsg_out[...] = grad_joined[:, feature:].astype(BF)


def fine_grad(cols, place, got, pool, cot, feats, message, w_in, w_out, bias, sum_rows):
    total, feature = cot.shape
    rows = 1024
    spec = pl.BlockSpec((rows, feature), lambda c: (c, 0))
    return pl.pallas_call(
        fine_grad_kernel,
        grid=(total // rows,),
        out_shape=(
            jax.ShapeDtypeStruct((total, feature), F32),
            jax.ShapeDtypeStruct((total, feature), BF),
            jax.ShapeDtypeStruct((sum_rows, feature), F32),
        ),
        in_specs=[SM, VM, VM, VM, spec, spec, spec, VM, VM, VM],
        out_specs=(spec, spec, VM),
        scratch_shapes=[pltpu.VMEM((total, feature), F32)],
        compiler_params=params(),
        cost_estimate=takes(19),
        name="fine_layer_backward",
    )(cols, place, got, pool, cot, feats, message, w_in, w_out, bias)


def spread_edge_kernel(cols, adj, gmsg, gx, rims_out, carry_out, acc, *, blocks):
    k = cols.shape[1]
    upper = pl.program_id(0) == 1
    width = rims_out.shape[0]
    first = jnp.where(upper, blocks - CHUNK, 0)
    acc[0:width, :] = jnp.zeros_like(gx)
    acc[width : 2 * width, :] = gx[...]
    acc[2 * width :, :] = jnp.zeros_like(gx)
    for j in range(CHUNK):
        spread_row(adj[j], cols, first + j, k, gmsg[j * BLK : (j + 1) * BLK, :], acc, first)

    @pl.when(jnp.logical_not(upper))
    def _():
        rims_out[...] = acc[0:width, :].astype(BF)
        carry_out[...] = acc[width:, :]

    @pl.when(upper)
    def _():
        rims_out[...] = acc[2 * width :, :].astype(BF)
        carry_out[...] = acc[0 : 2 * width, :]


def spread_edge(cols, adj, gmsg, gx):
    blocks, _, span = adj.shape
    feature = gmsg.shape[1]
    chunks = blocks // CHUNK
    return pl.pallas_call(
        functools.partial(spread_edge_kernel, blocks=blocks),
        grid=(2,),
        out_shape=(
            jax.ShapeDtypeStruct((2 * HALO, feature), BF),
            jax.ShapeDtypeStruct((4 * HALO, feature), F32),
        ),
        in_specs=[
            SM,
            pl.BlockSpec((CHUNK, BLK, span), lambda c: (c * (chunks - 1), 0, 0)),
            pl.BlockSpec((CHUNK * BLK, feature), lambda c: (c * (chunks - 1), 0)),
            pl.BlockSpec((CHUNK * BLK, feature), lambda c: (c * (chunks - 1), 0)),
        ],
        out_specs=(
            pl.BlockSpec((HALO, feature), lambda c: (c, 0)),
            pl.BlockSpec((2 * HALO, feature), lambda c: (c, 0)),
        ),
        scratch_shapes=[pltpu.VMEM((3 * HALO, feature), F32)],
        compiler_params=params(),
        cost_estimate=takes(3),
        name="spread_edge",
    )(cols, adj, gmsg, gx)


def spread_inner_kernel(cols, adj_a, adj_b, gmsg_a, gmsg_b, gx_a, gx_b, carry, mid_out, rims_out, acc, *, rim):
    k = cols.shape[1]
    step = pl.program_id(0)
    steps = pl.num_programs(0)
    width = rim * BLK
    total = mid_out.shape[0]

    @pl.when(step == 0)
    def _():
        acc[0 : 2 * width, :] = carry[0 : 2 * width, :]
        acc[2 * width : total - 2 * width, :] = jnp.zeros((total - 4 * width, acc.shape[1]), F32)
        acc[total - 2 * width :, :] = carry[2 * width :, :]

    for half, (adj, gmsg, gx) in enumerate(((adj_a, gmsg_a, gx_a), (adj_b, gmsg_b, gx_b))):
        chunk = 2 * step + 1 + half
        for j in range(CHUNK):
            spread_row(adj[j], cols, chunk * CHUNK + j, k, gmsg[j * BLK : (j + 1) * BLK, :], acc, rim)
        rows = gx.shape[0]
        acc[pl.ds(pl.multiple_of(chunk * rows, rows), rows), :] += gx[...]

    @pl.when(step == steps - 1)
    def _():
        mid_out[...] = acc[...].astype(BF)
        rims_out[0:width, :] = acc[0:width, :]
        rims_out[width:, :] = acc[total - width :, :]


def spread_inner(cols, adj, gmsg, gx, carry):
    total, feature = gx.shape
    blocks, _, span = adj.shape
    rows = CHUNK * BLK
    return pl.pallas_call(
        functools.partial(spread_inner_kernel, rim=HALO // BLK),
        grid=(blocks // CHUNK // 2 - 1,),
        out_shape=(
            jax.ShapeDtypeStruct((total, feature), BF),
            jax.ShapeDtypeStruct((2 * HALO, feature), F32),
        ),
        in_specs=[
            SM,
            pl.BlockSpec((CHUNK, BLK, span), lambda c: (2 * c + 1, 0, 0)),
            pl.BlockSpec((CHUNK, BLK, span), lambda c: (2 * c + 2, 0, 0)),
            pl.BlockSpec((rows, feature), lambda c: (2 * c + 1, 0)),
            pl.BlockSpec((rows, feature), lambda c: (2 * c + 2, 0)),
            pl.BlockSpec((rows, feature), lambda c: (2 * c + 1, 0)),
            pl.BlockSpec((rows, feature), lambda c: (2 * c + 2, 0)),
            VM,
        ],
        out_specs=(VM, VM),
        scratch_shapes=[pltpu.VMEM((total, feature), F32)],
        compiler_params=params(),
        cost_estimate=takes(18),
        name="spread_inner",
    )(cols, adj, adj, gmsg, gmsg, gx, gx, carry)


def rim_add_kernel(me, mid_in, rims, prev, after, out, *, groups):
    low = jnp.where(me[0] > 0, prev[...].astype(F32), 0.0)
    high = jnp.where(me[0] < groups - 1, after[...].astype(F32), 0.0)
    out[...] = (rims[...] + jnp.where(pl.program_id(0) == 0, low, high)).astype(BF)


def rim_add(me, groups, mid, rims, prev, after):
    total, feature = mid.shape
    return pl.pallas_call(
        functools.partial(rim_add_kernel, groups=groups),
        grid=(2,),
        out_shape=jax.ShapeDtypeStruct(mid.shape, BF),
        in_specs=[
            SM,
            pl.BlockSpec(memory_space=pl.ANY),
            pl.BlockSpec((HALO, feature), lambda c: (c, 0)),
            VM,
            VM,
        ],
        out_specs=pl.BlockSpec((HALO, feature), lambda c: (c * (total // HALO - 1), 0)),
        input_output_aliases={1: 0},
        compiler_params=params(),
        cost_estimate=takes(2),
        name="rim_add",
    )(me, mid, rims, prev, after)


def after_all(value, *others):
    return lax.optimization_barrier((value,) + others)[0]


def exchange(parts):
    return lax.all_to_all(parts, "grp", split_axis=0, concat_axis=0, tiled=True)


def gather_rows(rows):
    groups = lax.axis_size("grp")
    got = exchange(jnp.broadcast_to(rows[None], (groups,) + rows.shape))
    return got.reshape((groups * rows.shape[0],) + rows.shape[1:])


def halo_pair(low, high):
    count = lax.axis_size("grp")
    prev = lax.ppermute(high, "grp", [(i, (i + 1) % count) for i in range(count)])
    after = lax.ppermute(low, "grp", [((i + 1) % count, i) for i in range(count)])
    return prev, after


def hop_by(rows, axis, hop):
    return lax.ppermute(rows, axis, [(i, i ^ hop) for i in range(lax.axis_size(axis))])


def gather_hops(rows):
    groups = lax.axis_size("grp")
    if groups != 8:
        return [rows] + [hop_by(rows, "grp", hop) for hop in range(1, groups)]
    got = {hop: hop_by(rows, "grp", hop) for hop in (4, 2, 1)}
    got[5] = hop_by(got[4], "grp", 1)
    got[6] = hop_by(got[4], "grp", 2)
    got[3] = hop_by(got[2], "grp", 1)
    got[7] = hop_by(got[5], "grp", 2)
    return [rows] + [got[hop] for hop in range(1, 8)]


def add_low(*parts):
    return sum(part.astype(F32) for part in parts).astype(BF)


def scatter_hops(parts):
    groups = lax.axis_size("grp")
    if groups != 8:
        return [hop_by(parts[hop - 1], "grp", hop) for hop in range(1, groups)]
    far = hop_by(parts[6], "grp", 7)
    six = hop_by(parts[5], "grp", 2)
    five = hop_by(parts[4], "grp", 1)
    three = hop_by(parts[2], "grp", 1)
    return [
        hop_by(add_low(parts[3], five, six), "grp", 4),
        hop_by(add_low(parts[1], three), "grp", 2),
        hop_by(parts[0], "grp", 1),
        far,
    ]


ALL = ("slab", "grp")


def padded_rows(height):
    part = 8 * lax.axis_size(ALL)
    return -(-height // part) * part


def send_shares(rows):
    count = lax.axis_size(ALL)
    shares = rows.reshape(count, rows.shape[0] // count, rows.shape[1])
    return lax.all_to_all(shares, ALL, split_axis=0, concat_axis=0, tiled=True)


def share_sums(rows):
    count = lax.axis_size(ALL)
    return lax.all_to_all(
        jnp.broadcast_to(rows[None], (count,) + rows.shape), ALL, split_axis=0, concat_axis=0, tiled=True
    )


def body(
    node_feats,
    cotangent,
    fine_adjacency,
    fine_columns,
    pool_one,
    pool_one_columns,
    count_one,
    owner_one,
    adjacency_one,
    columns_one,
    pool_two,
    pool_two_columns,
    count_two,
    owner_two,
    adjacency_two,
    columns_two,
    weight_in,
    weight_out,
    biases,
):
    groups = lax.axis_size("grp")
    feature = node_feats.shape[1]
    slots_one = owner_one.shape[0]
    balance_one = slots_one // 2
    slots_two = owner_two.shape[0]
    me = lax.axis_index("grp").astype(jnp.int32).reshape(1)
    bias_rows = [biases[level : level + 1] for level in range(3)]

    cap_one = slots_one // groups
    place_one, mine_two, send = prep(
        count_one, pool_one_columns, count_two, owner_one.reshape(1, slots_one), owner_two.reshape(1, slots_two),
        columns_two.reshape(1, -1), pool_one, cotangent, adjacency_two, groups, balance_one,
    )
    prev, after = halo_pair(node_feats[:HALO], node_feats[-HALO:])
    first = exchange(send)
    chunks = fine_adjacency.shape[0] // CHUNK
    fine_weights = (fine_adjacency, weight_in[0], weight_out[0], bias_rows[0])
    done = fine_inner(after_all(fine_columns, send), node_feats, *fine_weights, 1, chunks - 1, ())
    message0, result0 = fine_edge(me, groups, fine_columns, node_feats, prev, after, *fine_weights, *done)
    sent_one = pool_pack(pool_one_columns, place_one, pool_one, result0)
    sent_one, first = lax.optimization_barrier((sent_one, first))
    got_one = exchange(sent_one.reshape(groups, cap_one, feature))
    own_one = place_rows(first, got_one, balance_one)
    grad_up_one, gslots_two, table_one = place_pool(
        pool_two_columns, after_all(first, own_one), pool_two, balance_one, cap_one
    )
    at = cap_one + 2 + 2 * slots_two // 128
    columns_two_all = first[:, at, : columns_two.size].astype(jnp.int32).reshape(-1, columns_two.shape[1])
    message_one, result1, slots_two_mine = one_forward(
        me, columns_one, pool_two_columns, gather_hops(own_one), gslots_two, adjacency_one, pool_two,
        weight_in[1], weight_out[1], bias_rows[1],
    )
    level = 3 * feature
    up_send, gx_one, coarse_sums, *parts_back = coarse_levels(
        me, columns_two_all, columns_one, pool_two_columns, gather_hops(slots_two_mine), mine_two, first,
        adjacency_one, pool_two, table_one, own_one, message_one, result1, grad_up_one,
        weight_in[1], weight_out[1], bias_rows[1], weight_in[2], weight_out[2], bias_rows[2],
        padded_rows(2 * level + 2),
    )
    up_got = exchange(up_send)
    grad_send = owner_sum(table_one, gx_one, scatter_hops(parts_back))
    grad_send, up_got = lax.optimization_barrier((grad_send, up_got))
    grad_got = exchange(grad_send)
    node_out = node_out_rows(pool_one_columns, place_one, up_got, pool_one, result0)
    grad_got, node_out = lax.optimization_barrier((grad_got, node_out))

    coarse_shares = send_shares(after_all(coarse_sums, grad_got))
    gx_zero, gmsg_zero, fine_sums = fine_grad(
        pool_one_columns, place_one, grad_got, pool_one, cotangent, node_feats, message0,
        weight_in[0], weight_out[0], bias_rows[0], padded_rows(level + 1),
    )
    coarse_shares, gmsg_zero, fine_sums = lax.optimization_barrier((coarse_shares, gmsg_zero, fine_sums))
    fine_shares = send_shares(fine_sums)
    rims_out, carry = spread_edge(fine_columns, fine_adjacency, gmsg_zero, gx_zero)
    fine_shares, carry = lax.optimization_barrier((fine_shares, carry))
    mine = jnp.concatenate([jnp.sum(fine_shares, axis=0), jnp.sum(coarse_shares, axis=0)], axis=0).astype(BF)
    sums = share_sums(mine).astype(F32)
    from_prev, from_after = halo_pair(rims_out[:HALO], rims_out[HALO:])
    mid, rims_own = spread_inner(fine_columns, fine_adjacency, gmsg_zero, gx_zero, after_all(carry, mine))
    grad_feats = rim_add(me, groups, mid, rims_own, from_prev, from_after)
    cut = fine_shares.shape[1]
    fine_sums = sums[:, :cut].reshape(-1, feature)
    coarse_sums = sums[:, cut:].reshape(-1, feature)

    scale = 1.0 / math.sqrt(node_feats.shape[0] * groups * lax.axis_size("slab"))
    wide = 2 * feature
    grad_in = jnp.stack([fine_sums[:wide], coarse_sums[:wide], coarse_sums[level : level + wide]])
    grad_out = jnp.stack([fine_sums[wide:level], coarse_sums[wide:level], coarse_sums[level + wide : 2 * level]])
    grad_bias = jnp.concatenate([fine_sums[level : level + 1], coarse_sums[2 * level : 2 * level + 2]])
    return (node_out, grad_feats, grad_in * scale, grad_out * scale, grad_bias * scale)


def solution(mesh):
    rows = P(("slab", "grp"), None)
    blocks = P(("slab", "grp"), None, None)
    flat = P(("slab", "grp"))
    placed = (
        rows, rows, blocks, rows, blocks, rows, flat, flat, blocks, rows,
        blocks, rows, flat, flat, blocks, rows, P(), P(), P(),
    )
    return jax.shard_map(
        body,
        mesh=mesh,
        in_specs=placed,
        out_specs=(rows, rows, P(), P(), P()),
        check_vma=False,
    )
```

```python
import functools
import math

import jax
import jax.numpy as jnp
from jax import lax
from jax.experimental import pallas as pl
from jax.experimental.pallas import tpu as pltpu
from jax.sharding import PartitionSpec as P

BF = jnp.bfloat16
F32 = jnp.float32
HALO = 512
BLK = 64
CHUNK = 8
EXTRA = 16
VMEM_LIMIT = 56 * 1024 * 1024

VM = pl.BlockSpec(memory_space=pltpu.VMEM)
SM = pl.BlockSpec(memory_space=pltpu.SMEM)


def params():
    return pltpu.CompilerParams(vmem_limit_bytes=VMEM_LIMIT)


def takes(microseconds):
    return pl.CostEstimate(flops=0, bytes_accessed=int(3 * microseconds * 3.69e6), transcendentals=0)


def dot(a, b):
    return jnp.dot(a, b, preferred_element_type=F32)


def dot_nt(a, b):
    return lax.dot_general(a, b, (((1,), (1,)), ((), ())), preferred_element_type=F32)


def dot_tn(a, b):
    return lax.dot_general(a, b, (((0,), (0,)), ((), ())), preferred_element_type=F32)


def iota(shape, dim):
    return lax.broadcasted_iota(jnp.int32, shape, dim)


def as_ones(mask):
    return jnp.where(mask, 1.0, 0.0).astype(BF)


def tile_at(ref, index):
    return ref[pl.ds(pl.multiple_of(index * BLK, BLK), BLK), :]


def apply_row(block, cols, r, count, ref, shift=0):
    picked = jnp.concatenate([tile_at(ref, cols[r, i] - shift) for i in range(count)], axis=0)
    return dot(block, picked)


def spread_row(block, cols, r, count, rows, acc, shift=0):
    spread = dot_tn(block, rows)
    for i in range(count):
        at = pl.ds(pl.multiple_of((cols[r, i] - shift) * BLK, BLK), BLK)
        acc[at, :] += spread[i * BLK : (i + 1) * BLK]


def place_matrix(row_table, first, count):
    n = row_table.shape[1]
    return as_ones(row_table == iota((count, n), 0) + first)


def digits(values):
    shifted = values + 1
    return (shifted >> 6).astype(F32), (shifted & 63).astype(F32)


def from_digits(high, low):
    return (high.astype(F32) * 64.0 + low.astype(F32)).astype(jnp.int32) - 1


def lane_rows(values):
    n = values.shape[1]
    rows = []
    for at in range(0, n, 128):
        row = values[:, at : min(at + 128, n)]
        if row.shape[1] < 128:
            row = jnp.concatenate([row, jnp.zeros((1, 128 - row.shape[1]), F32)], axis=1)
        rows.append(row)
    return rows


def pack_slots(
    count, count_two, owner_ref, two_ref, cols_two, rows_ref, place_cols_out, mine_out, send_out, groups, balance
):
    slots = owner_ref.shape[1]
    cap = slots // groups
    feature = rows_ref.shape[1] // 2
    owner = owner_ref[...]
    live = iota((1, slots), 1) < count[0]
    rows = max(16, groups)
    target = iota((rows, slots), 0)
    low = target * balance
    hit = (owner >= low) & (owner < low + balance) & live
    onehot = jnp.where(hit, 1.0, 0.0)
    upper = as_ones(iota((slots, slots), 0) <= iota((slots, slots), 1))
    running = dot(onehot.astype(BF), upper)
    rank = jnp.sum(onehot * running, axis=0, keepdims=True) - 1.0
    base = jnp.sum(jnp.where(hit, target * cap, 0).astype(F32), axis=0, keepdims=True)
    start = jnp.sum(jnp.where(hit, low, 0).astype(F32), axis=0, keepdims=True)
    place = jnp.where(live, (base + rank).astype(jnp.int32), slots)
    place_cols_out[...] = jnp.broadcast_to(place.astype(F32), (128, slots)).T
    two = two_ref[...]
    two = jnp.where(iota(two.shape, 1) < count_two[0], two, -1)
    mine_out[...] = two
    two_high, two_low = digits(two)
    shared = lane_rows(two_high) + lane_rows(two_low)
    for r in range(cols_two.shape[0]):
        shared = shared + lane_rows(cols_two[r : r + 1, :].astype(F32))
    local_high, local_low = digits(owner - start.astype(jnp.int32))
    kind = iota((rows, slots), 0)
    parts = jnp.where(kind == 0, local_high, jnp.where(kind == 1, local_low, 0.0)).astype(BF)
    for d in range(groups):
        ones = place_matrix(place, d * cap, cap)
        packed = dot(ones, rows_ref[...]).astype(BF)
        send_out[d, 0:cap, :] = packed[:, :feature]
        send_out[d, cap : 2 * cap, :] = packed[:, feature:]
        code = dot_nt(parts, ones)
        if cap < 128:
            code = jnp.concatenate([code, jnp.zeros((rows, 128 - cap), F32)], axis=1)
        tail = [code[0:1], code[1:2]] + shared
        tail = jnp.concatenate(tail + [jnp.zeros((EXTRA - len(tail), 128), F32)], axis=0)
        send_out[d, 2 * cap :, :] = tail.astype(BF)


def level_of(level, w_in, w_out, bias):
    return w_in.at[level], w_out.at[level], bias.at[pl.ds(level, 1), :]


def layer_rows(x, message, w_in, w_out, bias):
    pre = dot(jnp.concatenate([x, message], axis=1), w_in) + bias
    hidden = (pre * jax.nn.sigmoid(pre)).astype(BF)
    return (x.astype(F32) + dot(hidden, w_out)).astype(BF)


def fine_kernel(
    me, cols, pool_cols, count, count_two, prev, after, owner, two, cols_two, feats_hbm, adj_hbm, pool_hbm, cot_hbm,
    w_in, w_out, bias, msg_out, res_out, send_out, place_cols_out, mine_out,
    ext, adj, res, pool, cot, slots_scr, feats_sem, adj_sem, pool_sem, cot_sem, *, groups, balance,
):
    w_in, w_out, bias = level_of(0, w_in, w_out, bias)
    k = cols.shape[1]
    chunk = pl.program_id(0)
    rows = CHUNK * BLK
    width = prev.shape[0]
    chunks = adj.shape[0] // CHUNK

    def feats_copy(c):
        at = pl.multiple_of(c * rows, rows)
        return pltpu.make_async_copy(
            feats_hbm.at[pl.ds(at, rows), :], ext.at[pl.ds(width + at, rows), :], feats_sem.at[c]
        )

    def adj_copy(c):
        at = pl.ds(c * CHUNK, CHUNK)
        return pltpu.make_async_copy(adj_hbm.at[at], adj.at[at], adj_sem.at[c])

    def pool_copy():
        return pltpu.make_async_copy(pool_hbm, pool, pool_sem)

    def cot_copy():
        return pltpu.make_async_copy(cot_hbm, cot, cot_sem)

    @pl.when(chunk == 0)
    def _():
        feats_copy(0).start()
        for c in range(chunks):
            if c + 1 < chunks:
                feats_copy(c + 1).start()
            adj_copy(c).start()
        pool_copy().start()
        cot_copy().start()
        ext[0:width, :] = jnp.where(me[0] > 0, prev[...], jnp.zeros_like(prev))
        ext[width + chunks * rows :, :] = jnp.where(me[0] < groups - 1, after[...], jnp.zeros_like(after))
        feats_copy(0).wait()

    @pl.when(chunk + 1 < chunks)
    def _():
        feats_copy(chunk + 1).wait()

    @pl.when(chunk < chunks)
    def _():
        adj_copy(chunk).wait()
        for j in range(CHUNK):
            block = apply_row(adj[chunk * CHUNK + j], cols, chunk * CHUNK + j, k, ext)
            msg_out[j * BLK : (j + 1) * BLK, :] = block.astype(BF)
        x = ext[pl.ds(pl.multiple_of(width + chunk * rows, rows), rows), :]
        result = layer_rows(x, msg_out[...], w_in[...], w_out[...], bias[...])
        res_out[...] = result
        res[pl.ds(pl.multiple_of(chunk * rows, rows), rows), :] = result

    @pl.when(chunk == chunks)
    def _():
        pool_copy().wait()
        cot_copy().wait()
        k = pool_cols.shape[1]
        for q in range(pool.shape[0]):
            picked = [
                jnp.concatenate([tile_at(ref, pool_cols[q, i]) for i in range(k)], axis=0) for ref in (res, cot)
            ]
            slots_scr[q * BLK : (q + 1) * BLK, :] = dot(pool[q], jnp.concatenate(picked, axis=1)).astype(BF)
        pack_slots(
            count, count_two, owner, two, cols_two, slots_scr, place_cols_out, mine_out, send_out, groups, balance
        )


def fine_forward(
    me, cols, pool_cols, count, count_two, prev, after, owner, two, cols_two, feats, adj, pool, cot, w_in, w_out, bias,
    groups, balance,
):
    total, feature = feats.shape
    slots = owner.shape[1]
    rows = CHUNK * BLK
    chunks = total // rows
    hbm = pl.BlockSpec(memory_space=pl.ANY)
    spec = pl.BlockSpec((rows, feature), lambda c: (jnp.minimum(c, chunks - 1), 0))
    return pl.pallas_call(
        functools.partial(fine_kernel, groups=groups, balance=balance),
        grid=(chunks + 1,),
        out_shape=(
            jax.ShapeDtypeStruct((total, feature), BF),
            jax.ShapeDtypeStruct((total, feature), BF),
            jax.ShapeDtypeStruct((groups, 2 * (slots // groups) + EXTRA, feature), BF),
            jax.ShapeDtypeStruct((slots, 128), F32),
            jax.ShapeDtypeStruct(two.shape, jnp.int32),
        ),
        in_specs=[SM] * 5 + [VM] * 5 + [hbm] * 4 + [VM] * 3,
        out_specs=(spec, spec, VM, VM, VM),
        scratch_shapes=[
            pltpu.VMEM((total + 2 * HALO, feature), BF),
            pltpu.VMEM(adj.shape, BF),
            pltpu.VMEM((total, feature), BF),
            pltpu.VMEM(pool.shape, BF),
            pltpu.VMEM((total, feature), BF),
            pltpu.VMEM((slots, 2 * feature), BF),
            pltpu.SemaphoreType.DMA((chunks,)),
            pltpu.SemaphoreType.DMA((chunks,)),
            pltpu.SemaphoreType.DMA,
            pltpu.SemaphoreType.DMA,
        ],
        compiler_params=params(),
        cost_estimate=takes(20),
        name="fine_forward",
    )(
        me, cols, pool_cols, count, count_two, prev, after, owner, two, cols_two, feats, adj, pool, cot,
        w_in, w_out, bias,
    )


def place_all(tables, got, n, offset):
    cap = tables[0].shape[1]
    own = jnp.zeros((n, got.shape[2]), F32)
    for d in range(got.shape[0]):
        own += dot(place_matrix(tables[d], 0, n), got[d, offset : offset + cap, :])
    return own.astype(BF)


def tables_from(got, cap):
    at = 2 * cap
    return [from_digits(got[d, at : at + 1, :], got[d, at + 1 : at + 2, :])[:, :cap] for d in range(got.shape[0])]


def place_kernel(got, own_out):
    cap = (got.shape[1] - EXTRA) // 2
    own_out[...] = place_all(tables_from(got, cap), got, own_out.shape[0], 0)


def place_rows(got, balance):
    return pl.pallas_call(
        place_kernel,
        out_shape=jax.ShapeDtypeStruct((balance, got.shape[2]), BF),
        in_specs=[VM],
        out_specs=VM,
        compiler_params=params(),
        cost_estimate=takes(3),
        name="place_own_one",
    )(got)


def place_pool_kernel(cols, got, pool, own_out, slots_out, table_out):
    k = cols.shape[1]
    cap = table_out.shape[1]
    tables = tables_from(got, cap)
    own_out[...] = place_all(tables, got, own_out.shape[0], cap)
    for d in range(got.shape[0]):
        table_out[d : d + 1, :] = tables[d]
    for q in range(pool.shape[0]):
        slots_out[q * BLK : (q + 1) * BLK, :] = apply_row(pool[q], cols, q, k, own_out).astype(BF)


def place_pool(cols, got, pool, balance, cap):
    groups, _, feature = got.shape
    return pl.pallas_call(
        place_pool_kernel,
        out_shape=(
            jax.ShapeDtypeStruct((balance, feature), BF),
            jax.ShapeDtypeStruct((pool.shape[0] * BLK, feature), BF),
            jax.ShapeDtypeStruct((groups, cap), jnp.int32),
        ),
        in_specs=[SM, VM, VM],
        out_specs=(VM, VM, VM),
        compiler_params=params(),
        cost_estimate=takes(3),
        name="place_grad_up_one",
    )(cols, got, pool)


def one_forward_kernel(me, cols, pool_cols, *refs):
    pieces = refs[:-10]
    gslots, adj, pool, w_in, w_out, bias, msg_out, res_out, slots_out, ctx = refs[-10:]
    w_in, w_out, bias = level_of(1, w_in, w_out, bias)
    own = pieces[0]
    n = own.shape[0]
    for hop, piece in enumerate(pieces):
        ctx[pl.ds(pl.multiple_of((me[0] ^ hop) * n, n), n), :] = piece[...]
    k = cols.shape[1]
    for r in range(adj.shape[0]):
        msg_out[r * BLK : (r + 1) * BLK, :] = apply_row(adj[r], cols, r, k, ctx).astype(BF)
    res_out[...] = layer_rows(own[...], msg_out[...], w_in[...], w_out[...], bias[...])
    k = pool_cols.shape[1]
    for q in range(pool.shape[0]):
        rows = apply_row(pool[q], pool_cols, q, k, res_out).astype(BF)
        slots_out[q * BLK : (q + 1) * BLK, 0 : rows.shape[1]] = rows
    slots_out[:, own.shape[1] :] = gslots[...]


def one_forward(me, cols, pool_cols, pieces, gslots, adj, pool, w_in, w_out, bias):
    own = pieces[0]
    own_shape = jax.ShapeDtypeStruct(own.shape, BF)
    return pl.pallas_call(
        one_forward_kernel,
        out_shape=(own_shape, own_shape, jax.ShapeDtypeStruct((gslots.shape[0], 2 * own.shape[1]), BF)),
        in_specs=[SM, SM, SM] + [VM] * (len(pieces) + 6),
        out_specs=(VM, VM, VM),
        scratch_shapes=[pltpu.VMEM((len(pieces) * own.shape[0], own.shape[1]), BF)],
        compiler_params=params(),
        cost_estimate=takes(3),
        name="level_one_forward",
    )(me, cols, pool_cols, *pieces, gslots, adj, pool, w_in, w_out, bias)


def grad_pre_rows(grad_low, x, message, w_in, w_out, bias):
    joined = jnp.concatenate([x, message], axis=1)
    pre = dot(joined, w_in) + bias
    sig = jax.nn.sigmoid(pre)
    hidden = (pre * sig).astype(BF)
    grad_pre = dot_nt(grad_low, w_out) * (sig * (1.0 + pre * (1.0 - sig)))
    return joined, hidden, grad_pre


def coarse_kernel(groups, me, cols_two, cols_one, pool_cols, *refs):
    slots_two, refs = refs[:groups], refs[groups:]
    adj_pieces, refs = refs[:groups], refs[groups:]
    (
        mine_two, first, adj_one, pool_two, table_one, own_one, msg_one, res_one, gup_one,
        w_in, w_out, bias, up_out, gx_out, sums_out,
    ) = refs[:15]
    part_outs, refs = refs[15 : 15 + groups - 1], refs[15 + groups - 1 :]
    both, adj_two, xs, gs, ms, hs, gps, rs, ctx_acc, up_acc, gmsg, gctx_acc = refs
    wi1, wo1, b1 = level_of(1, w_in, w_out, bias)
    wi2, wo2, b2 = level_of(2, w_in, w_out, bias)
    feature = own_one.shape[1]
    n2 = xs.shape[0]
    n1 = own_one.shape[0]
    slots = mine_two.shape[1]
    per = adj_two.shape[0] // groups
    for hop in range(groups):
        source = me[0] ^ hop
        both[pl.ds(pl.multiple_of(source * slots, slots), slots), :] = slots_two[hop][...]
        adj_two[pl.ds(source * per, per)] = adj_pieces[hop][...]
    cap = table_one.shape[1]
    lanes = slots // 128
    at = 2 * cap + 2
    table = jnp.concatenate(
        [
            from_digits(first[d, at + c : at + c + 1, :], first[d, at + lanes + c : at + lanes + c + 1, :])
            for d in range(first.shape[0])
            for c in range(lanes)
        ],
        axis=1,
    )
    step = min(256, n2)
    for v in range(0, n2, step):
        rows = dot(place_matrix(table, v, step), both[...]).astype(BF)
        xs[v : v + step, :] = rows[:, :feature]
        gs[v : v + step, :] = rows[:, feature:]
    k = cols_two.shape[1]
    for r in range(n2 // BLK):
        ms[r * BLK : (r + 1) * BLK, :] = apply_row(adj_two[r], cols_two, r, k, xs).astype(BF)
    ctx_acc[...] = jnp.zeros_like(ctx_acc)
    for v in range(0, n2, step):
        x, m, g = xs[v : v + step, :], ms[v : v + step, :], gs[v : v + step, :]
        joined, hidden, grad_pre = grad_pre_rows(g, x, m, wi2[...], wo2[...], b2[...])
        rs[v : v + step, :feature] = (x.astype(F32) + dot(hidden, wo2[...])).astype(BF)
        hs[v : v + step, :] = hidden
        gps[v : v + step, :] = grad_pre
        grad_joined = dot_nt(grad_pre.astype(BF), wi2[...])
        ctx_acc[v : v + step, :] += g.astype(F32) + grad_joined[:, :feature]
        gm = grad_joined[:, feature:].astype(BF)
        for j in range(step // BLK):
            r = v // BLK + j
            spread_row(adj_two[r], cols_two, r, k, gm[j * BLK : (j + 1) * BLK], ctx_acc)
    rs[:, feature:] = ctx_acc[...].astype(BF)
    balance = slots // 2
    at = pl.ds(pl.multiple_of(me[0] * balance, balance), balance)
    gp_own = gps[at, :]
    joined = jnp.concatenate([xs[at, :], ms[at, :]], axis=1)
    level = 3 * feature
    sums_out[level : level + 2 * feature, :] = dot_tn(joined, gp_own.astype(BF))
    sums_out[level + 2 * feature : 2 * level, :] = dot_tn(hs[at, :], gs[at, :])
    bias_two = jnp.sum(gp_own, axis=0, keepdims=True)
    mine = place_matrix(mine_two[...], 0, n2)
    back = dot_tn(mine, rs[...]).astype(BF)
    up_acc[:, :feature] = res_one[...].astype(F32)
    up_acc[:, feature:] = gup_one[...].astype(F32)
    k = pool_cols.shape[1]
    for q in range(pool_two.shape[0]):
        spread_row(pool_two[q], pool_cols, q, k, back[q * BLK : (q + 1) * BLK], up_acc)
    up_low = up_acc[:, :feature].astype(BF)
    for d in range(table_one.shape[0]):
        up_out[d] = dot_tn(place_matrix(table_one[d : d + 1, :], 0, n1), up_low).astype(BF)
    grad = up_acc[:, feature:]
    grad_low = grad.astype(BF)
    joined, hidden, grad_pre = grad_pre_rows(grad_low, own_one[...], msg_one[...], wi1[...], wo1[...], b1[...])
    grad_pre_low = grad_pre.astype(BF)
    sums_out[0 : 2 * feature, :] = dot_tn(joined, grad_pre_low)
    sums_out[2 * feature : level, :] = dot_tn(hidden, grad_low)
    bias_one = jnp.sum(grad_pre, axis=0, keepdims=True)
    rest = sums_out.shape[0] - 2 * level
    row = iota((rest, feature), 0)
    sums_out[2 * level :, :] = jnp.where(row == 0, bias_one, jnp.where(row == 1, bias_two, 0.0))
    grad_joined = dot_nt(grad_pre_low, wi1[...])
    gmsg[...] = grad_joined[:, feature:].astype(BF)
    gctx_acc[...] = jnp.zeros_like(gctx_acc)
    k = cols_one.shape[1]
    for r in range(adj_one.shape[0]):
        spread_row(adj_one[r], cols_one, r, k, gmsg[r * BLK : (r + 1) * BLK, :], gctx_acc)
    own_at = pl.ds(pl.multiple_of(me[0] * n1, n1), n1)
    gx_out[...] = grad + grad_joined[:, :feature] + gctx_acc[own_at, :]
    for hop in range(1, groups):
        at = pl.ds(pl.multiple_of((me[0] ^ hop) * n1, n1), n1)
        part_outs[hop - 1][...] = gctx_acc[at, :].astype(BF)


def coarse_levels(
    me, cols_two, cols_one, pool_cols, slots_two, adj_two, mine_two, first, adj_one, pool_two,
    table_one, own_one, msg_one, res_one, gup_one, w_in, w_out, bias, sum_rows,
):
    groups = len(slots_two)
    n1, feature = own_one.shape
    n2 = mine_two.shape[1] // 2 * groups
    cap = table_one.shape[1]
    return pl.pallas_call(
        functools.partial(coarse_kernel, groups),
        out_shape=(
            jax.ShapeDtypeStruct((groups, cap, feature), BF),
            jax.ShapeDtypeStruct((n1, feature), F32),
            jax.ShapeDtypeStruct((sum_rows, feature), F32),
        )
        + (jax.ShapeDtypeStruct((n1, feature), BF),) * (groups - 1),
        in_specs=[SM] * 4 + [VM] * (12 + 2 * groups),
        out_specs=(VM,) * (2 + groups),
        scratch_shapes=[
            pltpu.VMEM((groups * mine_two.shape[1], 2 * feature), BF),
            pltpu.VMEM((n2 // BLK, BLK, cols_two.shape[1] * BLK), BF),
            pltpu.VMEM((n2, feature), BF),
            pltpu.VMEM((n2, feature), BF),
            pltpu.VMEM((n2, feature), BF),
            pltpu.VMEM((n2, feature), BF),
            pltpu.VMEM((n2, feature), F32),
            pltpu.VMEM((n2, 2 * feature), BF),
            pltpu.VMEM((n2, feature), F32),
            pltpu.VMEM((n1, 2 * feature), F32),
            pltpu.VMEM((n1, feature), BF),
            pltpu.VMEM((groups * n1, feature), F32),
        ],
        compiler_params=params(),
        cost_estimate=takes(9),
        name="coarse_levels",
    )(
        me, cols_two, cols_one, pool_cols, *slots_two, *adj_two, mine_two, first, adj_one, pool_two,
        table_one, own_one, msg_one, res_one, gup_one, w_in, w_out, bias,
    )


def owner_sum_kernel(table, gx, *refs):
    send_out = refs[-1]
    total = gx[...]
    for part in refs[:-1]:
        total += part[...].astype(F32)
    low = total.astype(BF)
    for d in range(table.shape[0]):
        send_out[d] = dot_tn(place_matrix(table[d : d + 1, :], 0, gx.shape[0]), low).astype(BF)


def owner_sum(table, gx, parts):
    return pl.pallas_call(
        owner_sum_kernel,
        out_shape=jax.ShapeDtypeStruct(table.shape + (gx.shape[1],), BF),
        in_specs=[VM] * (2 + len(parts)),
        out_specs=VM,
        compiler_params=params(),
        cost_estimate=takes(3),
        name="grad_own_one_send",
    )(table, gx, *parts)


def lift(place, got, pool, cols, acc):
    groups, height, _ = got.shape
    cap = place.shape[0] // groups
    packed = jnp.concatenate([got[d, height - cap :, :] for d in range(groups)], axis=0)
    count = packed.shape[0]
    ones = as_ones(place[:, 0:1].astype(jnp.int32) == iota((place.shape[0], count), 1))
    rows = dot(ones, packed).astype(BF)
    k = cols.shape[1]
    for q in range(pool.shape[0]):
        spread_row(pool[q], cols, q, k, rows[q * BLK : (q + 1) * BLK], acc)


def node_out_kernel(cols, place, got, pool, base, out, acc):
    rows = out.shape[0]

    @pl.when(pl.program_id(0) == 0)
    def _():
        acc[...] = jnp.zeros_like(acc)
        lift(place, got, pool, cols, acc)

    at = pl.ds(pl.multiple_of(pl.program_id(0) * rows, rows), rows)
    out[...] = (base[...].astype(F32) + acc[at, :]).astype(BF)


def node_out_rows(cols, place, got, pool, base):
    total, feature = base.shape
    rows = 1024
    spec = pl.BlockSpec((rows, feature), lambda c: (c, 0))
    return pl.pallas_call(
        node_out_kernel,
        grid=(total // rows,),
        out_shape=jax.ShapeDtypeStruct((total, feature), BF),
        in_specs=[SM, VM, VM, VM, spec],
        out_specs=spec,
        scratch_shapes=[pltpu.VMEM((total, feature), F32)],
        compiler_params=params(),
        cost_estimate=takes(9),
        name="node_out",
    )(cols, place, got, pool, base)


def fine_grad_kernel(
    cols, place, got, pool, coarse, cot, feats, message, w_in, w_out, bias, gx_out, gmsg_out, send_out, sums, acc
):
    w_in, w_out, bias = level_of(0, w_in, w_out, bias)
    rows = cot.shape[0]
    feature = cot.shape[1]

    @pl.when(pl.program_id(0) == 0)
    def _():
        acc[...] = jnp.zeros_like(acc)
        sums[...] = jnp.zeros_like(sums)
        lift(place, got, pool, cols, acc)

    at = pl.ds(pl.multiple_of(pl.program_id(0) * rows, rows), rows)
    grad = cot[...].astype(F32) + acc[at, :]
    grad_low = grad.astype(BF)
    joined, hidden, grad_pre = grad_pre_rows(grad_low, feats[...], message[...], w_in[...], w_out[...], bias[...])
    grad_pre_low = grad_pre.astype(BF)
    level = 3 * feature
    sums[0 : 2 * feature, :] += dot_tn(joined, grad_pre_low)
    sums[2 * feature : level, :] += dot_tn(hidden, grad_low)
    sums[level : level + 1, :] += jnp.sum(grad_pre, axis=0, keepdims=True)
    grad_joined = dot_nt(grad_pre_low, w_in[...])
    gx_out[...] = grad + grad_joined[:, :feature]
    gmsg_out[...] = grad_joined[:, feature:].astype(BF)

    @pl.when(pl.program_id(0) == pl.num_programs(0) - 1)
    def _():
        count = send_out.shape[0]
        cut = sums.shape[0] // count
        send_out[:, :cut, :] = sums[...].astype(BF).reshape(count, cut, feature)
        send_out[:, cut:, :] = coarse[...].astype(BF).reshape(count, coarse.shape[0] // count, feature)


def fine_grad(cols, place, got, pool, coarse, cot, feats, message, w_in, w_out, bias, sum_rows, count):
    total, feature = cot.shape
    rows = 1024
    spec = pl.BlockSpec((rows, feature), lambda c: (c, 0))
    return pl.pallas_call(
        fine_grad_kernel,
        grid=(total // rows,),
        out_shape=(
            jax.ShapeDtypeStruct((total, feature), F32),
            jax.ShapeDtypeStruct((total, feature), BF),
            jax.ShapeDtypeStruct((count, (sum_rows + coarse.shape[0]) // count, feature), BF),
        ),
        in_specs=[SM, VM, VM, VM, VM, spec, spec, spec, VM, VM, VM],
        out_specs=(spec, spec, VM),
        scratch_shapes=[pltpu.VMEM((sum_rows, feature), F32), pltpu.VMEM((total, feature), F32)],
        compiler_params=params(),
        cost_estimate=takes(19),
        name="fine_layer_backward",
    )(cols, place, got, pool, coarse, cot, feats, message, w_in, w_out, bias)


def spread_edge_kernel(cols, adj, gmsg, gx, low_out, high_out, carry_out, acc, *, blocks):
    k = cols.shape[1]
    upper = pl.program_id(0) == 1
    width = low_out.shape[0]
    first = jnp.where(upper, blocks - CHUNK, 0)
    acc[0:width, :] = jnp.zeros_like(gx)
    acc[width : 2 * width, :] = gx[...]
    acc[2 * width :, :] = jnp.zeros_like(gx)
    for j in range(CHUNK):
        spread_row(adj[j], cols, first + j, k, gmsg[j * BLK : (j + 1) * BLK, :], acc, first)

    @pl.when(jnp.logical_not(upper))
    def _():
        low_out[...] = acc[0:width, :].astype(BF)
        carry_out[...] = acc[width:, :]

    @pl.when(upper)
    def _():
        high_out[...] = acc[2 * width :, :].astype(BF)
        carry_out[...] = acc[0 : 2 * width, :]


def spread_edge(cols, adj, gmsg, gx):
    blocks, _, span = adj.shape
    feature = gmsg.shape[1]
    chunks = blocks // CHUNK
    return pl.pallas_call(
        functools.partial(spread_edge_kernel, blocks=blocks),
        grid=(2,),
        out_shape=(
            jax.ShapeDtypeStruct((HALO, feature), BF),
            jax.ShapeDtypeStruct((HALO, feature), BF),
            jax.ShapeDtypeStruct((4 * HALO, feature), F32),
        ),
        in_specs=[
            SM,
            pl.BlockSpec((CHUNK, BLK, span), lambda c: (c * (chunks - 1), 0, 0)),
            pl.BlockSpec((CHUNK * BLK, feature), lambda c: (c * (chunks - 1), 0)),
            pl.BlockSpec((CHUNK * BLK, feature), lambda c: (c * (chunks - 1), 0)),
        ],
        out_specs=(
            VM,
            VM,
            pl.BlockSpec((2 * HALO, feature), lambda c: (c, 0)),
        ),
        scratch_shapes=[pltpu.VMEM((3 * HALO, feature), F32)],
        compiler_params=params(),
        cost_estimate=takes(3),
        name="spread_edge",
    )(cols, adj, gmsg, gx)


def spread_inner_kernel(
    me, cols, adj_a, adj_b, gmsg_a, gmsg_b, gx_a, gx_b, carry, prev, after, mid_out, acc, *, rim, groups
):
    k = cols.shape[1]
    step = pl.program_id(0)
    steps = pl.num_programs(0)
    width = rim * BLK
    total = mid_out.shape[0]

    @pl.when(step == 0)
    def _():
        acc[0 : 2 * width, :] = carry[0 : 2 * width, :]
        acc[2 * width : total - 2 * width, :] = jnp.zeros((total - 4 * width, acc.shape[1]), F32)
        acc[total - 2 * width :, :] = carry[2 * width :, :]
        acc[0:width, :] += jnp.where(me[0] > 0, prev[...].astype(F32), 0.0)
        acc[total - width :, :] += jnp.where(me[0] < groups - 1, after[...].astype(F32), 0.0)

    for half, (adj, gmsg, gx) in enumerate(((adj_a, gmsg_a, gx_a), (adj_b, gmsg_b, gx_b))):
        chunk = 2 * step + 1 + half
        for j in range(CHUNK):
            spread_row(adj[j], cols, chunk * CHUNK + j, k, gmsg[j * BLK : (j + 1) * BLK, :], acc, rim)
        rows = gx.shape[0]
        acc[pl.ds(pl.multiple_of(chunk * rows, rows), rows), :] += gx[...]

    @pl.when(step == steps - 1)
    def _():
        mid_out[...] = acc[...].astype(BF)


def spread_inner(me, groups, cols, adj, gmsg, gx, carry, prev, after):
    total, feature = gx.shape
    blocks, _, span = adj.shape
    rows = CHUNK * BLK
    return pl.pallas_call(
        functools.partial(spread_inner_kernel, rim=HALO // BLK, groups=groups),
        grid=(blocks // CHUNK // 2 - 1,),
        out_shape=jax.ShapeDtypeStruct((total, feature), BF),
        in_specs=[
            SM,
            SM,
            pl.BlockSpec((CHUNK, BLK, span), lambda c: (2 * c + 1, 0, 0)),
            pl.BlockSpec((CHUNK, BLK, span), lambda c: (2 * c + 2, 0, 0)),
            pl.BlockSpec((rows, feature), lambda c: (2 * c + 1, 0)),
            pl.BlockSpec((rows, feature), lambda c: (2 * c + 2, 0)),
            pl.BlockSpec((rows, feature), lambda c: (2 * c + 1, 0)),
            pl.BlockSpec((rows, feature), lambda c: (2 * c + 2, 0)),
            VM,
            VM,
            VM,
        ],
        out_specs=VM,
        scratch_shapes=[pltpu.VMEM((total, feature), F32)],
        compiler_params=params(),
        cost_estimate=takes(18),
        name="spread_inner",
    )(me, cols, adj, adj, gmsg, gmsg, gx, gx, carry, prev, after)


def scale_kernel(sums, in_out, out_out, bias_out, *, cut, scale):
    count, height, feature = sums.shape
    level = 3 * feature
    fine = sums[:, :cut, :].reshape(count * cut, feature).astype(F32) * scale
    coarse = sums[:, cut:, :].reshape(count * (height - cut), feature).astype(F32) * scale
    for at, rows in enumerate((fine, coarse, coarse[level:])):
        in_out[at] = rows[: 2 * feature]
        out_out[at] = rows[2 * feature : level]
    bias_out[0:1, :] = fine[level : level + 1]
    bias_out[1:3, :] = coarse[2 * level : 2 * level + 2]


def scaled_sums(sums, cut, scale):
    feature = sums.shape[2]
    return pl.pallas_call(
        functools.partial(scale_kernel, cut=cut, scale=scale),
        out_shape=(
            jax.ShapeDtypeStruct((3, 2 * feature, feature), F32),
            jax.ShapeDtypeStruct((3, feature, feature), F32),
            jax.ShapeDtypeStruct((3, feature), F32),
        ),
        in_specs=[VM],
        out_specs=(VM, VM, VM),
        compiler_params=params(),
        cost_estimate=takes(1),
        name="scaled_sums",
    )(sums)


def after_all(value, *others):
    return lax.optimization_barrier((value,) + others)[0]


def exchange(parts):
    return lax.all_to_all(parts, "grp", split_axis=0, concat_axis=0, tiled=True)


def gather_rows(rows):
    groups = lax.axis_size("grp")
    got = exchange(jnp.broadcast_to(rows[None], (groups,) + rows.shape))
    return got.reshape((groups * rows.shape[0],) + rows.shape[1:])


def halo_pair(low, high):
    count = lax.axis_size("grp")
    prev = lax.ppermute(high, "grp", [(i, (i + 1) % count) for i in range(count)])
    after = lax.ppermute(low, "grp", [((i + 1) % count, i) for i in range(count)])
    return prev, after


def hop_by(rows, axis, hop):
    return lax.ppermute(rows, axis, [(i, i ^ hop) for i in range(lax.axis_size(axis))])


def gather_near(rows):
    groups = lax.axis_size("grp")
    hops = (4, 2, 1) if groups == 8 else range(1, groups)
    return {hop: hop_by(rows, "grp", hop) for hop in hops}


def gather_far(rows, near):
    groups = lax.axis_size("grp")
    got = dict(near)
    if groups == 8:
        got[5] = hop_by(got[4], "grp", 1)
        got[6] = hop_by(got[4], "grp", 2)
        got[3] = hop_by(got[2], "grp", 1)
        got[7] = hop_by(got[5], "grp", 2)
    return [rows] + [got[hop] for hop in range(1, groups)]


def gather_hops(rows):
    return gather_far(rows, gather_near(rows))


def add_low(*parts):
    return sum(part.astype(F32) for part in parts).astype(BF)


def scatter_hops(parts):
    groups = lax.axis_size("grp")
    if groups != 8:
        return [hop_by(parts[hop - 1], "grp", hop) for hop in range(1, groups)]
    far = hop_by(parts[6], "grp", 7)
    six = hop_by(parts[5], "grp", 2)
    five = hop_by(parts[4], "grp", 1)
    three = hop_by(parts[2], "grp", 1)
    return [
        hop_by(add_low(parts[3], five, six), "grp", 4),
        hop_by(add_low(parts[1], three), "grp", 2),
        hop_by(parts[0], "grp", 1),
        far,
    ]


ALL = ("slab", "grp")


def padded_rows(height):
    part = 16 * lax.axis_size(ALL)
    return -(-height // part) * part


def send_shares(shares):
    return lax.all_to_all(shares, ALL, split_axis=0, concat_axis=0, tiled=True)


def share_sums(rows):
    count = lax.axis_size(ALL)
    return lax.all_to_all(
        jnp.broadcast_to(rows[None], (count,) + rows.shape), ALL, split_axis=0, concat_axis=0, tiled=True
    )


def body(
    node_feats,
    cotangent,
    fine_adjacency,
    fine_columns,
    pool_one,
    pool_one_columns,
    count_one,
    owner_one,
    adjacency_one,
    columns_one,
    pool_two,
    pool_two_columns,
    count_two,
    owner_two,
    adjacency_two,
    columns_two,
    weight_in,
    weight_out,
    biases,
):
    groups = lax.axis_size("grp")
    feature = node_feats.shape[1]
    slots_one = owner_one.shape[0]
    balance_one = slots_one // 2
    slots_two = owner_two.shape[0]
    me = lax.axis_index("grp").astype(jnp.int32).reshape(1)
    weights = (weight_in, weight_out, biases)

    cap_one = slots_one // groups
    prev, after = halo_pair(node_feats[:HALO], node_feats[-HALO:])
    near_two = gather_near(adjacency_two)
    message0, result0, sent_one, place_cols, mine_two = fine_forward(
        me, fine_columns, pool_one_columns, count_one, count_two, prev, after, owner_one.reshape(1, slots_one),
        owner_two.reshape(1, slots_two), columns_two, node_feats, fine_adjacency, pool_one, cotangent, *weights,
        groups, balance_one,
    )
    hops = sorted(near_two)
    sent_one, *near_two = lax.optimization_barrier((sent_one, *[near_two[hop] for hop in hops]))
    adj_two = gather_far(adjacency_two, dict(zip(hops, near_two)))
    first = exchange(sent_one)
    own_one = place_rows(first, balance_one)
    grad_up_one, gslots_two, table_one = place_pool(
        pool_two_columns, after_all(first, own_one), pool_two, balance_one, cap_one
    )
    at = 2 * cap_one + 2 + 2 * slots_two // 128
    columns_two_all = first[:, at : at + columns_two.shape[0], : columns_two.shape[1]].astype(jnp.int32)
    columns_two_all = columns_two_all.reshape(-1, columns_two.shape[1])
    message_one, result1, slots_two_mine = one_forward(
        me, columns_one, pool_two_columns, gather_hops(own_one), gslots_two, adjacency_one, pool_two,
        *weights,
    )
    level = 3 * feature
    up_send, gx_one, coarse_sums, *parts_back = coarse_levels(
        me, columns_two_all, columns_one, pool_two_columns, gather_hops(slots_two_mine), adj_two, mine_two, first,
        adjacency_one, pool_two, table_one, own_one, message_one, result1, grad_up_one,
        *weights, padded_rows(2 * level + 2),
    )
    up_got = exchange(up_send)
    grad_send = owner_sum(table_one, gx_one, scatter_hops(parts_back))
    grad_send, up_got = lax.optimization_barrier((grad_send, up_got))
    grad_got = exchange(grad_send)
    node_out = node_out_rows(pool_one_columns, place_cols, up_got, pool_one, result0)
    grad_got, node_out = lax.optimization_barrier((grad_got, node_out))

    sum_rows = padded_rows(level + 1)
    gx_zero, gmsg_zero, sums_send = fine_grad(
        pool_one_columns, place_cols, grad_got, pool_one, coarse_sums, cotangent, node_feats, message0, *weights,
        sum_rows, lax.axis_size(ALL),
    )
    shares = send_shares(sums_send)
    rim_low, rim_high, carry = spread_edge(fine_columns, fine_adjacency, gmsg_zero, gx_zero)
    from_prev, from_after = halo_pair(rim_low, rim_high)
    shares, from_prev, from_after = lax.optimization_barrier((shares, from_prev, from_after))
    mine = jnp.sum(shares.astype(F32), axis=0).astype(BF)
    sums = share_sums(mine)
    from_prev = after_all(from_prev, mine)
    grad_feats = spread_inner(
        me, groups, fine_columns, fine_adjacency, gmsg_zero, gx_zero, carry, from_prev, from_after
    )
    scale = 1.0 / math.sqrt(node_feats.shape[0] * groups * lax.axis_size("slab"))
    return (node_out, grad_feats, *scaled_sums(sums, sum_rows // lax.axis_size(ALL), scale))


def solution(mesh):
    rows = P(("slab", "grp"), None)
    blocks = P(("slab", "grp"), None, None)
    flat = P(("slab", "grp"))
    placed = (
        rows, rows, blocks, rows, blocks, rows, flat, flat, blocks, rows,
        blocks, rows, flat, flat, blocks, rows, P(), P(), P(),
    )
    return jax.shard_map(
        body,
        mesh=mesh,
        in_specs=placed,
        out_specs=(rows, rows, P(), P(), P()),
        check_vma=False,
    )
```

```python
import functools
import math

import jax
import jax.numpy as jnp
from jax import lax
from jax.experimental import pallas as pl
from jax.experimental.pallas import tpu as pltpu
from jax.sharding import PartitionSpec as P

BF = jnp.bfloat16
F32 = jnp.float32
HALO = 512
BLK = 64
CHUNK = 8
EXTRA = 16
VMEM_LIMIT = 56 * 1024 * 1024

VM = pl.BlockSpec(memory_space=pltpu.VMEM)
SM = pl.BlockSpec(memory_space=pltpu.SMEM)


def params():
    return pltpu.CompilerParams(vmem_limit_bytes=VMEM_LIMIT)


def takes(microseconds):
    return pl.CostEstimate(flops=0, bytes_accessed=int(3 * microseconds * 3.69e6), transcendentals=0)


def dot(a, b):
    return jnp.dot(a, b, preferred_element_type=F32)


def dot_nt(a, b):
    return lax.dot_general(a, b, (((1,), (1,)), ((), ())), preferred_element_type=F32)


def dot_tn(a, b):
    return lax.dot_general(a, b, (((0,), (0,)), ((), ())), preferred_element_type=F32)


def iota(shape, dim):
    return lax.broadcasted_iota(jnp.int32, shape, dim)


def as_ones(mask):
    return jnp.where(mask, 1.0, 0.0).astype(BF)


def tile_at(ref, index):
    return ref[pl.ds(pl.multiple_of(index * BLK, BLK), BLK), :]


def apply_row(block, cols, r, count, ref, shift=0):
    picked = jnp.concatenate([tile_at(ref, cols[r, i] - shift) for i in range(count)], axis=0)
    return dot(block, picked)


def spread_row(block, cols, r, count, rows, acc, shift=0):
    spread = dot_tn(block, rows)
    for i in range(count):
        at = pl.ds(pl.multiple_of((cols[r, i] - shift) * BLK, BLK), BLK)
        acc[at, :] += spread[i * BLK : (i + 1) * BLK]


def place_matrix(row_table, first, count):
    n = row_table.shape[1]
    return as_ones(row_table == iota((count, n), 0) + first)


def digits(values):
    shifted = values + 1
    return (shifted >> 6).astype(F32), (shifted & 63).astype(F32)


def from_digits(high, low):
    return (high.astype(F32) * 64.0 + low.astype(F32)).astype(jnp.int32) - 1


def lane_rows(values):
    n = values.shape[1]
    rows = []
    for at in range(0, n, 128):
        row = values[:, at : min(at + 128, n)]
        if row.shape[1] < 128:
            row = jnp.concatenate([row, jnp.zeros((1, 128 - row.shape[1]), F32)], axis=1)
        rows.append(row)
    return rows


def pack_slots(
    count, count_two, owner_ref, two_ref, cols_two, rows_ref, place_cols_out, mine_out, send_out, groups, balance
):
    slots = owner_ref.shape[1]
    cap = slots // groups
    feature = rows_ref.shape[1] // 2
    owner = owner_ref[...]
    live = iota((1, slots), 1) < count[0]
    rows = max(16, groups)
    target = iota((rows, slots), 0)
    low = target * balance
    hit = (owner >= low) & (owner < low + balance) & live
    onehot = jnp.where(hit, 1.0, 0.0)
    upper = as_ones(iota((slots, slots), 0) <= iota((slots, slots), 1))
    running = dot(onehot.astype(BF), upper)
    rank = jnp.sum(onehot * running, axis=0, keepdims=True) - 1.0
    base = jnp.sum(jnp.where(hit, target * cap, 0).astype(F32), axis=0, keepdims=True)
    start = jnp.sum(jnp.where(hit, low, 0).astype(F32), axis=0, keepdims=True)
    place = jnp.where(live, (base + rank).astype(jnp.int32), slots)
    place_cols_out[...] = jnp.broadcast_to(place.astype(F32), (128, slots)).T
    two = two_ref[...]
    two = jnp.where(iota(two.shape, 1) < count_two[0], two, -1)
    mine_out[...] = two
    two_high, two_low = digits(two)
    shared = lane_rows(two_high) + lane_rows(two_low)
    for r in range(cols_two.shape[0]):
        shared = shared + lane_rows(cols_two[r : r + 1, :].astype(F32))
    local_high, local_low = digits(owner - start.astype(jnp.int32))
    kind = iota((rows, slots), 0)
    parts = jnp.where(kind == 0, local_high, jnp.where(kind == 1, local_low, 0.0)).astype(BF)
    for d in range(groups):
        ones = place_matrix(place, d * cap, cap)
        packed = dot(ones, rows_ref[...]).astype(BF)
        send_out[d, 0:cap, :] = packed[:, :feature]
        send_out[d, cap : 2 * cap, :] = packed[:, feature:]
        code = dot_nt(parts, ones)
        if cap < 128:
            code = jnp.concatenate([code, jnp.zeros((rows, 128 - cap), F32)], axis=1)
        tail = [code[0:1], code[1:2]] + shared
        tail = jnp.concatenate(tail + [jnp.zeros((EXTRA - len(tail), 128), F32)], axis=0)
        send_out[d, 2 * cap :, :] = tail.astype(BF)


def level_of(level, w_in, w_out, bias):
    return w_in.at[level], w_out.at[level], bias.at[pl.ds(level, 1), :]


def layer_rows(x, message, w_in, w_out, bias):
    pre = dot(jnp.concatenate([x, message], axis=1), w_in) + bias
    hidden = (pre * jax.nn.sigmoid(pre)).astype(BF)
    return (x.astype(F32) + dot(hidden, w_out)).astype(BF)


def fine_kernel(
    me, cols, pool_cols, count, count_two, prev, after, owner, two, cols_two, feats_hbm, adj_hbm, pool_hbm, cot_hbm,
    w_in, w_out, bias, msg_out, res_out, send_out, place_cols_out, mine_out,
    ext, adj, res, pool, cot, slots_scr, feats_sem, adj_sem, pool_sem, cot_sem, *, groups, balance,
):
    w_in, w_out, bias = level_of(0, w_in, w_out, bias)
    k = cols.shape[1]
    chunk = pl.program_id(0)
    rows = CHUNK * BLK
    width = prev.shape[0]
    chunks = adj.shape[0] // CHUNK

    def feats_copy(c):
        at = pl.multiple_of(c * rows, rows)
        return pltpu.make_async_copy(
            feats_hbm.at[pl.ds(at, rows), :], ext.at[pl.ds(width + at, rows), :], feats_sem.at[c]
        )

    def adj_copy(c):
        at = pl.ds(c * CHUNK, CHUNK)
        return pltpu.make_async_copy(adj_hbm.at[at], adj.at[at], adj_sem.at[c])

    def pool_copy():
        return pltpu.make_async_copy(pool_hbm, pool, pool_sem)

    def cot_copy():
        return pltpu.make_async_copy(cot_hbm, cot, cot_sem)

    @pl.when(chunk == 0)
    def _():
        feats_copy(0).start()
        for c in range(chunks):
            if c + 1 < chunks:
                feats_copy(c + 1).start()
            adj_copy(c).start()
        pool_copy().start()
        cot_copy().start()
        ext[0:width, :] = jnp.where(me[0] > 0, prev[...], jnp.zeros_like(prev))
        ext[width + chunks * rows :, :] = jnp.where(me[0] < groups - 1, after[...], jnp.zeros_like(after))
        feats_copy(0).wait()

    @pl.when(chunk + 1 < chunks)
    def _():
        feats_copy(chunk + 1).wait()

    @pl.when(chunk < chunks)
    def _():
        adj_copy(chunk).wait()
        for j in range(CHUNK):
            block = apply_row(adj[chunk * CHUNK + j], cols, chunk * CHUNK + j, k, ext)
            msg_out[j * BLK : (j + 1) * BLK, :] = block.astype(BF)
        x = ext[pl.ds(pl.multiple_of(width + chunk * rows, rows), rows), :]
        result = layer_rows(x, msg_out[...], w_in[...], w_out[...], bias[...])
        res_out[...] = result
        res[pl.ds(pl.multiple_of(chunk * rows, rows), rows), :] = result

    @pl.when(chunk == chunks)
    def _():
        pool_copy().wait()
        cot_copy().wait()
        k = pool_cols.shape[1]
        for q in range(pool.shape[0]):
            picked = [
                jnp.concatenate([tile_at(ref, pool_cols[q, i]) for i in range(k)], axis=0) for ref in (res, cot)
            ]
            slots_scr[q * BLK : (q + 1) * BLK, :] = dot(pool[q], jnp.concatenate(picked, axis=1)).astype(BF)
        pack_slots(
            count, count_two, owner, two, cols_two, slots_scr, place_cols_out, mine_out, send_out, groups, balance
        )


def fine_forward(
    me, cols, pool_cols, count, count_two, prev, after, owner, two, cols_two, feats, adj, pool, cot, w_in, w_out, bias,
    groups, balance,
):
    total, feature = feats.shape
    slots = owner.shape[1]
    rows = CHUNK * BLK
    chunks = total // rows
    hbm = pl.BlockSpec(memory_space=pl.ANY)
    spec = pl.BlockSpec((rows, feature), lambda c: (jnp.minimum(c, chunks - 1), 0))
    return pl.pallas_call(
        functools.partial(fine_kernel, groups=groups, balance=balance),
        grid=(chunks + 1,),
        out_shape=(
            jax.ShapeDtypeStruct((total, feature), BF),
            jax.ShapeDtypeStruct((total, feature), BF),
            jax.ShapeDtypeStruct((groups, 2 * (slots // groups) + EXTRA, feature), BF),
            jax.ShapeDtypeStruct((slots, 128), F32),
            jax.ShapeDtypeStruct(two.shape, jnp.int32),
        ),
        in_specs=[SM] * 5 + [VM] * 5 + [hbm] * 4 + [VM] * 3,
        out_specs=(spec, spec, VM, VM, VM),
        scratch_shapes=[
            pltpu.VMEM((total + 2 * HALO, feature), BF),
            pltpu.VMEM(adj.shape, BF),
            pltpu.VMEM((total, feature), BF),
            pltpu.VMEM(pool.shape, BF),
            pltpu.VMEM((total, feature), BF),
            pltpu.VMEM((slots, 2 * feature), BF),
            pltpu.SemaphoreType.DMA((chunks,)),
            pltpu.SemaphoreType.DMA((chunks,)),
            pltpu.SemaphoreType.DMA,
            pltpu.SemaphoreType.DMA,
        ],
        compiler_params=params(),
        cost_estimate=takes(20),
        name="fine_forward",
    )(
        me, cols, pool_cols, count, count_two, prev, after, owner, two, cols_two, feats, adj, pool, cot,
        w_in, w_out, bias,
    )


def place_all(tables, got, n, offset):
    cap = tables[0].shape[1]
    own = jnp.zeros((n, got.shape[2]), F32)
    for d in range(got.shape[0]):
        own += dot(place_matrix(tables[d], 0, n), got[d, offset : offset + cap, :])
    return own.astype(BF)


def tables_from(got, cap):
    at = 2 * cap
    return [from_digits(got[d, at : at + 1, :], got[d, at + 1 : at + 2, :])[:, :cap] for d in range(got.shape[0])]


def place_kernel(got, own_out):
    cap = (got.shape[1] - EXTRA) // 2
    own_out[...] = place_all(tables_from(got, cap), got, own_out.shape[0], 0)


def place_rows(got, balance):
    return pl.pallas_call(
        place_kernel,
        out_shape=jax.ShapeDtypeStruct((balance, got.shape[2]), BF),
        in_specs=[VM],
        out_specs=VM,
        compiler_params=params(),
        cost_estimate=takes(3),
        name="place_own_one",
    )(got)


def place_pool_kernel(cols, got, pool, own_out, slots_out, table_out):
    k = cols.shape[1]
    cap = table_out.shape[1]
    tables = tables_from(got, cap)
    own_out[...] = place_all(tables, got, own_out.shape[0], cap)
    for d in range(got.shape[0]):
        table_out[d : d + 1, :] = tables[d]
    for q in range(pool.shape[0]):
        slots_out[q * BLK : (q + 1) * BLK, :] = apply_row(pool[q], cols, q, k, own_out).astype(BF)


def place_pool(cols, got, pool, balance, cap):
    groups, _, feature = got.shape
    return pl.pallas_call(
        place_pool_kernel,
        out_shape=(
            jax.ShapeDtypeStruct((balance, feature), BF),
            jax.ShapeDtypeStruct((pool.shape[0] * BLK, feature), BF),
            jax.ShapeDtypeStruct((groups, cap), jnp.int32),
        ),
        in_specs=[SM, VM, VM],
        out_specs=(VM, VM, VM),
        compiler_params=params(),
        cost_estimate=takes(3),
        name="place_grad_up_one",
    )(cols, got, pool)


def one_forward_kernel(me, cols, pool_cols, *refs):
    pieces = refs[:-10]
    gslots, adj, pool, w_in, w_out, bias, msg_out, res_out, slots_out, ctx = refs[-10:]
    w_in, w_out, bias = level_of(1, w_in, w_out, bias)
    own = pieces[0]
    n = own.shape[0]
    for hop, piece in enumerate(pieces):
        ctx[pl.ds(pl.multiple_of((me[0] ^ hop) * n, n), n), :] = piece[...]
    k = cols.shape[1]
    for r in range(adj.shape[0]):
        msg_out[r * BLK : (r + 1) * BLK, :] = apply_row(adj[r], cols, r, k, ctx).astype(BF)
    res_out[...] = layer_rows(own[...], msg_out[...], w_in[...], w_out[...], bias[...])
    k = pool_cols.shape[1]
    for q in range(pool.shape[0]):
        rows = apply_row(pool[q], pool_cols, q, k, res_out).astype(BF)
        slots_out[q * BLK : (q + 1) * BLK, 0 : rows.shape[1]] = rows
    slots_out[:, own.shape[1] :] = gslots[...]


def one_forward(me, cols, pool_cols, pieces, gslots, adj, pool, w_in, w_out, bias):
    own = pieces[0]
    own_shape = jax.ShapeDtypeStruct(own.shape, BF)
    return pl.pallas_call(
        one_forward_kernel,
        out_shape=(own_shape, own_shape, jax.ShapeDtypeStruct((gslots.shape[0], 2 * own.shape[1]), BF)),
        in_specs=[SM, SM, SM] + [VM] * (len(pieces) + 6),
        out_specs=(VM, VM, VM),
        scratch_shapes=[pltpu.VMEM((len(pieces) * own.shape[0], own.shape[1]), BF)],
        compiler_params=params(),
        cost_estimate=takes(3),
        name="level_one_forward",
    )(me, cols, pool_cols, *pieces, gslots, adj, pool, w_in, w_out, bias)


def grad_pre_rows(grad_low, x, message, w_in, w_out, bias):
    joined = jnp.concatenate([x, message], axis=1)
    pre = dot(joined, w_in) + bias
    sig = jax.nn.sigmoid(pre)
    hidden = (pre * sig).astype(BF)
    grad_pre = dot_nt(grad_low, w_out) * (sig * (1.0 + pre * (1.0 - sig)))
    return joined, hidden, grad_pre


def coarse_kernel(groups, me, cols_two, cols_one, pool_cols, *refs):
    slots_two, refs = refs[:groups], refs[groups:]
    adj_pieces, refs = refs[:groups], refs[groups:]
    (
        mine_two, first, adj_one, pool_two, table_one, own_one, msg_one, res_one, gup_one,
        w_in, w_out, bias, up_out, gx_out, sums_out,
    ) = refs[:15]
    part_outs, refs = refs[15 : 15 + groups - 1], refs[15 + groups - 1 :]
    both, adj_two, xs, gs, ms, hs, gps, rs, ctx_acc, up_acc, gmsg, gctx_acc = refs
    wi1, wo1, b1 = level_of(1, w_in, w_out, bias)
    wi2, wo2, b2 = level_of(2, w_in, w_out, bias)
    feature = own_one.shape[1]
    n2 = xs.shape[0]
    n1 = own_one.shape[0]
    slots = mine_two.shape[1]
    per = adj_two.shape[0] // groups
    for hop in range(groups):
        source = me[0] ^ hop
        both[pl.ds(pl.multiple_of(source * slots, slots), slots), :] = slots_two[hop][...]
        adj_two[pl.ds(source * per, per)] = adj_pieces[hop][...]
    cap = table_one.shape[1]
    lanes = slots // 128
    at = 2 * cap + 2
    table = jnp.concatenate(
        [
            from_digits(first[d, at + c : at + c + 1, :], first[d, at + lanes + c : at + lanes + c + 1, :])
            for d in range(first.shape[0])
            for c in range(lanes)
        ],
        axis=1,
    )
    step = min(256, n2)
    for v in range(0, n2, step):
        rows = dot(place_matrix(table, v, step), both[...]).astype(BF)
        xs[v : v + step, :] = rows[:, :feature]
        gs[v : v + step, :] = rows[:, feature:]
    k = cols_two.shape[1]
    for r in range(n2 // BLK):
        ms[r * BLK : (r + 1) * BLK, :] = apply_row(adj_two[r], cols_two, r, k, xs).astype(BF)
    ctx_acc[...] = jnp.zeros_like(ctx_acc)
    for v in range(0, n2, step):
        x, m, g = xs[v : v + step, :], ms[v : v + step, :], gs[v : v + step, :]
        joined, hidden, grad_pre = grad_pre_rows(g, x, m, wi2[...], wo2[...], b2[...])
        rs[v : v + step, :feature] = (x.astype(F32) + dot(hidden, wo2[...])).astype(BF)
        hs[v : v + step, :] = hidden
        gps[v : v + step, :] = grad_pre
        grad_joined = dot_nt(grad_pre.astype(BF), wi2[...])
        ctx_acc[v : v + step, :] += g.astype(F32) + grad_joined[:, :feature]
        gm = grad_joined[:, feature:].astype(BF)
        for j in range(step // BLK):
            r = v // BLK + j
            spread_row(adj_two[r], cols_two, r, k, gm[j * BLK : (j + 1) * BLK], ctx_acc)
    rs[:, feature:] = ctx_acc[...].astype(BF)
    balance = slots // 2
    at = pl.ds(pl.multiple_of(me[0] * balance, balance), balance)
    gp_own = gps[at, :]
    joined = jnp.concatenate([xs[at, :], ms[at, :]], axis=1)
    level = 3 * feature
    sums_out[level : level + 2 * feature, :] = dot_tn(joined, gp_own.astype(BF))
    sums_out[level + 2 * feature : 2 * level, :] = dot_tn(hs[at, :], gs[at, :])
    bias_two = jnp.sum(gp_own, axis=0, keepdims=True)
    mine = place_matrix(mine_two[...], 0, n2)
    back = dot_tn(mine, rs[...]).astype(BF)
    up_acc[:, :feature] = res_one[...].astype(F32)
    up_acc[:, feature:] = gup_one[...].astype(F32)
    k = pool_cols.shape[1]
    for q in range(pool_two.shape[0]):
        spread_row(pool_two[q], pool_cols, q, k, back[q * BLK : (q + 1) * BLK], up_acc)
    up_low = up_acc[:, :feature].astype(BF)
    for d in range(table_one.shape[0]):
        up_out[d] = dot_tn(place_matrix(table_one[d : d + 1, :], 0, n1), up_low).astype(BF)
    grad = up_acc[:, feature:]
    grad_low = grad.astype(BF)
    joined, hidden, grad_pre = grad_pre_rows(grad_low, own_one[...], msg_one[...], wi1[...], wo1[...], b1[...])
    grad_pre_low = grad_pre.astype(BF)
    sums_out[0 : 2 * feature, :] = dot_tn(joined, grad_pre_low)
    sums_out[2 * feature : level, :] = dot_tn(hidden, grad_low)
    bias_one = jnp.sum(grad_pre, axis=0, keepdims=True)
    rest = sums_out.shape[0] - 2 * level
    row = iota((rest, feature), 0)
    sums_out[2 * level :, :] = jnp.where(row == 0, bias_one, jnp.where(row == 1, bias_two, 0.0))
    grad_joined = dot_nt(grad_pre_low, wi1[...])
    gmsg[...] = grad_joined[:, feature:].astype(BF)
    gctx_acc[...] = jnp.zeros_like(gctx_acc)
    k = cols_one.shape[1]
    for r in range(adj_one.shape[0]):
        spread_row(adj_one[r], cols_one, r, k, gmsg[r * BLK : (r + 1) * BLK, :], gctx_acc)
    own_at = pl.ds(pl.multiple_of(me[0] * n1, n1), n1)
    gx_out[...] = grad + grad_joined[:, :feature] + gctx_acc[own_at, :]
    for hop in range(1, groups):
        at = pl.ds(pl.multiple_of((me[0] ^ hop) * n1, n1), n1)
        part_outs[hop - 1][...] = gctx_acc[at, :].astype(BF)


def coarse_levels(
    me, cols_two, cols_one, pool_cols, slots_two, adj_two, mine_two, first, adj_one, pool_two,
    table_one, own_one, msg_one, res_one, gup_one, w_in, w_out, bias, sum_rows,
):
    groups = len(slots_two)
    n1, feature = own_one.shape
    n2 = mine_two.shape[1] // 2 * groups
    cap = table_one.shape[1]
    return pl.pallas_call(
        functools.partial(coarse_kernel, groups),
        out_shape=(
            jax.ShapeDtypeStruct((groups, cap, feature), BF),
            jax.ShapeDtypeStruct((n1, feature), F32),
            jax.ShapeDtypeStruct((sum_rows, feature), F32),
        )
        + (jax.ShapeDtypeStruct((n1, feature), BF),) * (groups - 1),
        in_specs=[SM] * 4 + [VM] * (12 + 2 * groups),
        out_specs=(VM,) * (2 + groups),
        scratch_shapes=[
            pltpu.VMEM((groups * mine_two.shape[1], 2 * feature), BF),
            pltpu.VMEM((n2 // BLK, BLK, cols_two.shape[1] * BLK), BF),
            pltpu.VMEM((n2, feature), BF),
            pltpu.VMEM((n2, feature), BF),
            pltpu.VMEM((n2, feature), BF),
            pltpu.VMEM((n2, feature), BF),
            pltpu.VMEM((n2, feature), F32),
            pltpu.VMEM((n2, 2 * feature), BF),
            pltpu.VMEM((n2, feature), F32),
            pltpu.VMEM((n1, 2 * feature), F32),
            pltpu.VMEM((n1, feature), BF),
            pltpu.VMEM((groups * n1, feature), F32),
        ],
        compiler_params=params(),
        cost_estimate=takes(9),
        name="coarse_levels",
    )(
        me, cols_two, cols_one, pool_cols, *slots_two, *adj_two, mine_two, first, adj_one, pool_two,
        table_one, own_one, msg_one, res_one, gup_one, w_in, w_out, bias,
    )


def owner_sum_kernel(table, gx, *refs):
    send_out = refs[-1]
    total = gx[...]
    for part in refs[:-1]:
        total += part[...].astype(F32)
    low = total.astype(BF)
    for d in range(table.shape[0]):
        send_out[d] = dot_tn(place_matrix(table[d : d + 1, :], 0, gx.shape[0]), low).astype(BF)


def owner_sum(table, gx, parts):
    return pl.pallas_call(
        owner_sum_kernel,
        out_shape=jax.ShapeDtypeStruct(table.shape + (gx.shape[1],), BF),
        in_specs=[VM] * (2 + len(parts)),
        out_specs=VM,
        compiler_params=params(),
        cost_estimate=takes(3),
        name="grad_own_one_send",
    )(table, gx, *parts)


def lift(place, got, pool, cols, acc):
    groups, height, _ = got.shape
    cap = place.shape[0] // groups
    packed = jnp.concatenate([got[d, height - cap :, :] for d in range(groups)], axis=0)
    count = packed.shape[0]
    ones = as_ones(place[:, 0:1].astype(jnp.int32) == iota((place.shape[0], count), 1))
    rows = dot(ones, packed).astype(BF)
    k = cols.shape[1]
    for q in range(pool.shape[0]):
        spread_row(pool[q], cols, q, k, rows[q * BLK : (q + 1) * BLK], acc)


def node_out_kernel(cols, place, got, pool, base, out, acc):
    rows = out.shape[0]

    @pl.when(pl.program_id(0) == 0)
    def _():
        acc[...] = jnp.zeros_like(acc)
        lift(place, got, pool, cols, acc)

    at = pl.ds(pl.multiple_of(pl.program_id(0) * rows, rows), rows)
    out[...] = (base[...].astype(F32) + acc[at, :]).astype(BF)


def node_out_rows(cols, place, got, pool, base):
    total, feature = base.shape
    rows = 1024
    spec = pl.BlockSpec((rows, feature), lambda c: (c, 0))
    return pl.pallas_call(
        node_out_kernel,
        grid=(total // rows,),
        out_shape=jax.ShapeDtypeStruct((total, feature), BF),
        in_specs=[SM, VM, VM, VM, spec],
        out_specs=spec,
        scratch_shapes=[pltpu.VMEM((total, feature), F32)],
        compiler_params=params(),
        cost_estimate=takes(9),
        name="node_out",
    )(cols, place, got, pool, base)


def fine_grad_kernel(
    cols, place, got, pool, coarse, cot, feats, message, w_in, w_out, bias, gx_out, gmsg_out, send_out, sums, acc
):
    w_in, w_out, bias = level_of(0, w_in, w_out, bias)
    rows = cot.shape[0]
    feature = cot.shape[1]

    @pl.when(pl.program_id(0) == 0)
    def _():
        acc[...] = jnp.zeros_like(acc)
        sums[...] = jnp.zeros_like(sums)
        lift(place, got, pool, cols, acc)

    at = pl.ds(pl.multiple_of(pl.program_id(0) * rows, rows), rows)
    grad = cot[...].astype(F32) + acc[at, :]
    grad_low = grad.astype(BF)
    joined, hidden, grad_pre = grad_pre_rows(grad_low, feats[...], message[...], w_in[...], w_out[...], bias[...])
    grad_pre_low = grad_pre.astype(BF)
    level = 3 * feature
    sums[0 : 2 * feature, :] += dot_tn(joined, grad_pre_low)
    sums[2 * feature : level, :] += dot_tn(hidden, grad_low)
    sums[level : level + 1, :] += jnp.sum(grad_pre, axis=0, keepdims=True)
    grad_joined = dot_nt(grad_pre_low, w_in[...])
    gx_out[...] = grad + grad_joined[:, :feature]
    gmsg_out[...] = grad_joined[:, feature:].astype(BF)

    @pl.when(pl.program_id(0) == pl.num_programs(0) - 1)
    def _():
        count = send_out.shape[0]
        cut = sums.shape[0] // count
        send_out[:, :cut, :] = sums[...].astype(BF).reshape(count, cut, feature)
        send_out[:, cut:, :] = coarse[...].astype(BF).reshape(count, coarse.shape[0] // count, feature)


def fine_grad(cols, place, got, pool, coarse, cot, feats, message, w_in, w_out, bias, sum_rows, count):
    total, feature = cot.shape
    rows = 1024
    spec = pl.BlockSpec((rows, feature), lambda c: (c, 0))
    return pl.pallas_call(
        fine_grad_kernel,
        grid=(total // rows,),
        out_shape=(
            jax.ShapeDtypeStruct((total, feature), F32),
            jax.ShapeDtypeStruct((total, feature), BF),
            jax.ShapeDtypeStruct((count, (sum_rows + coarse.shape[0]) // count, feature), BF),
        ),
        in_specs=[SM, VM, VM, VM, VM, spec, spec, spec, VM, VM, VM],
        out_specs=(spec, spec, VM),
        scratch_shapes=[pltpu.VMEM((sum_rows, feature), F32), pltpu.VMEM((total, feature), F32)],
        compiler_params=params(),
        cost_estimate=takes(19),
        name="fine_layer_backward",
    )(cols, place, got, pool, coarse, cot, feats, message, w_in, w_out, bias)


def spread_edge_kernel(cols, adj, gmsg, gx, low_out, high_out, carry_out, acc, *, blocks):
    k = cols.shape[1]
    upper = pl.program_id(0) == 1
    width = low_out.shape[0]
    first = jnp.where(upper, blocks - CHUNK, 0)
    acc[0:width, :] = jnp.zeros_like(gx)
    acc[width : 2 * width, :] = gx[...]
    acc[2 * width :, :] = jnp.zeros_like(gx)
    for j in range(CHUNK):
        spread_row(adj[j], cols, first + j, k, gmsg[j * BLK : (j + 1) * BLK, :], acc, first)

    @pl.when(jnp.logical_not(upper))
    def _():
        low_out[...] = acc[0:width, :].astype(BF)
        carry_out[...] = acc[width:, :]

    @pl.when(upper)
    def _():
        high_out[...] = acc[2 * width :, :].astype(BF)
        carry_out[...] = acc[0 : 2 * width, :]


def spread_edge(cols, adj, gmsg, gx):
    blocks, _, span = adj.shape
    feature = gmsg.shape[1]
    chunks = blocks // CHUNK
    return pl.pallas_call(
        functools.partial(spread_edge_kernel, blocks=blocks),
        grid=(2,),
        out_shape=(
            jax.ShapeDtypeStruct((HALO, feature), BF),
            jax.ShapeDtypeStruct((HALO, feature), BF),
            jax.ShapeDtypeStruct((4 * HALO, feature), F32),
        ),
        in_specs=[
            SM,
            pl.BlockSpec((CHUNK, BLK, span), lambda c: (c * (chunks - 1), 0, 0)),
            pl.BlockSpec((CHUNK * BLK, feature), lambda c: (c * (chunks - 1), 0)),
            pl.BlockSpec((CHUNK * BLK, feature), lambda c: (c * (chunks - 1), 0)),
        ],
        out_specs=(
            VM,
            VM,
            pl.BlockSpec((2 * HALO, feature), lambda c: (c, 0)),
        ),
        scratch_shapes=[pltpu.VMEM((3 * HALO, feature), F32)],
        compiler_params=params(),
        cost_estimate=takes(3),
        name="spread_edge",
    )(cols, adj, gmsg, gx)


def spread_inner_kernel(
    me, cols, adj_a, adj_b, gmsg_a, gmsg_b, gx_a, gx_b, carry, prev, after, mid_out, acc, *, rim, groups
):
    k = cols.shape[1]
    step = pl.program_id(0)
    steps = pl.num_programs(0)
    width = rim * BLK
    total = mid_out.shape[0]

    @pl.when(step == 0)
    def _():
        acc[0 : 2 * width, :] = carry[0 : 2 * width, :]
        acc[2 * width : total - 2 * width, :] = jnp.zeros((total - 4 * width, acc.shape[1]), F32)
        acc[total - 2 * width :, :] = carry[2 * width :, :]
        acc[0:width, :] += jnp.where(me[0] > 0, prev[...].astype(F32), 0.0)
        acc[total - width :, :] += jnp.where(me[0] < groups - 1, after[...].astype(F32), 0.0)

    for half, (adj, gmsg, gx) in enumerate(((adj_a, gmsg_a, gx_a), (adj_b, gmsg_b, gx_b))):
        chunk = 2 * step + 1 + half
        for j in range(CHUNK):
            spread_row(adj[j], cols, chunk * CHUNK + j, k, gmsg[j * BLK : (j + 1) * BLK, :], acc, rim)
        rows = gx.shape[0]
        acc[pl.ds(pl.multiple_of(chunk * rows, rows), rows), :] += gx[...]

    @pl.when(step == steps - 1)
    def _():
        mid_out[...] = acc[...].astype(BF)


def spread_inner(me, groups, cols, adj, gmsg, gx, carry, prev, after):
    total, feature = gx.shape
    blocks, _, span = adj.shape
    rows = CHUNK * BLK
    return pl.pallas_call(
        functools.partial(spread_inner_kernel, rim=HALO // BLK, groups=groups),
        grid=(blocks // CHUNK // 2 - 1,),
        out_shape=jax.ShapeDtypeStruct((total, feature), BF),
        in_specs=[
            SM,
            SM,
            pl.BlockSpec((CHUNK, BLK, span), lambda c: (2 * c + 1, 0, 0)),
            pl.BlockSpec((CHUNK, BLK, span), lambda c: (2 * c + 2, 0, 0)),
            pl.BlockSpec((rows, feature), lambda c: (2 * c + 1, 0)),
            pl.BlockSpec((rows, feature), lambda c: (2 * c + 2, 0)),
            pl.BlockSpec((rows, feature), lambda c: (2 * c + 1, 0)),
            pl.BlockSpec((rows, feature), lambda c: (2 * c + 2, 0)),
            VM,
            VM,
            VM,
        ],
        out_specs=VM,
        scratch_shapes=[pltpu.VMEM((total, feature), F32)],
        compiler_params=params(),
        cost_estimate=takes(18),
        name="spread_inner",
    )(me, cols, adj, adj, gmsg, gmsg, gx, gx, carry, prev, after)


def scale_kernel(sums, in_out, out_out, bias_out, *, cut, scale):
    count, height, feature = sums.shape
    level = 3 * feature
    fine = sums[:, :cut, :].reshape(count * cut, feature).astype(F32) * scale
    coarse = sums[:, cut:, :].reshape(count * (height - cut), feature).astype(F32) * scale
    for at, rows in enumerate((fine, coarse, coarse[level:])):
        in_out[at] = rows[: 2 * feature]
        out_out[at] = rows[2 * feature : level]
    bias_out[0:1, :] = fine[level : level + 1]
    bias_out[1:3, :] = coarse[2 * level : 2 * level + 2]


def scaled_sums(sums, cut, scale):
    feature = sums.shape[2]
    return pl.pallas_call(
        functools.partial(scale_kernel, cut=cut, scale=scale),
        out_shape=(
            jax.ShapeDtypeStruct((3, 2 * feature, feature), F32),
            jax.ShapeDtypeStruct((3, feature, feature), F32),
            jax.ShapeDtypeStruct((3, feature), F32),
        ),
        in_specs=[VM],
        out_specs=(VM, VM, VM),
        compiler_params=params(),
        cost_estimate=takes(1),
        name="scaled_sums",
    )(sums)


def after_all(value, *others):
    return lax.optimization_barrier((value,) + others)[0]


def exchange(parts):
    return lax.all_to_all(parts, "grp", split_axis=0, concat_axis=0, tiled=True)


def gather_rows(rows):
    groups = lax.axis_size("grp")
    got = exchange(jnp.broadcast_to(rows[None], (groups,) + rows.shape))
    return got.reshape((groups * rows.shape[0],) + rows.shape[1:])


def halo_pair(low, high):
    count = lax.axis_size("grp")
    prev = lax.ppermute(high, "grp", [(i, (i + 1) % count) for i in range(count)])
    after = lax.ppermute(low, "grp", [((i + 1) % count, i) for i in range(count)])
    return prev, after


def hop_by(rows, axis, hop):
    return lax.ppermute(rows, axis, [(i, i ^ hop) for i in range(lax.axis_size(axis))])


def gather_near(rows):
    groups = lax.axis_size("grp")
    hops = (4, 2, 1) if groups == 8 else range(1, groups)
    return {hop: hop_by(rows, "grp", hop) for hop in hops}


def gather_far(rows, near):
    groups = lax.axis_size("grp")
    got = dict(near)
    if groups == 8:
        got[5] = hop_by(got[4], "grp", 1)
        got[6] = hop_by(got[4], "grp", 2)
        got[3] = hop_by(got[2], "grp", 1)
        got[7] = hop_by(got[5], "grp", 2)
    return [rows] + [got[hop] for hop in range(1, groups)]


def gather_hops(rows):
    return gather_far(rows, gather_near(rows))


def add_low(*parts):
    return sum(part.astype(F32) for part in parts).astype(BF)


def scatter_hops(parts):
    groups = lax.axis_size("grp")
    if groups != 8:
        return [hop_by(parts[hop - 1], "grp", hop) for hop in range(1, groups)]
    far = hop_by(parts[6], "grp", 7)
    six = hop_by(parts[5], "grp", 2)
    five = hop_by(parts[4], "grp", 1)
    three = hop_by(parts[2], "grp", 1)
    return [
        hop_by(add_low(parts[3], five, six), "grp", 4),
        hop_by(add_low(parts[1], three), "grp", 2),
        hop_by(parts[0], "grp", 1),
        far,
    ]


ALL = ("slab", "grp")


def padded_rows(height):
    part = 16 * lax.axis_size(ALL)
    return -(-height // part) * part


def send_shares(shares):
    return lax.all_to_all(shares, ALL, split_axis=0, concat_axis=0, tiled=True)


def share_sums(rows):
    count = lax.axis_size(ALL)
    return lax.all_to_all(
        jnp.broadcast_to(rows[None], (count,) + rows.shape), ALL, split_axis=0, concat_axis=0, tiled=True
    )


def body(
    node_feats,
    cotangent,
    fine_adjacency,
    fine_columns,
    pool_one,
    pool_one_columns,
    count_one,
    owner_one,
    adjacency_one,
    columns_one,
    pool_two,
    pool_two_columns,
    count_two,
    owner_two,
    adjacency_two,
    columns_two,
    weight_in,
    weight_out,
    biases,
):
    groups = lax.axis_size("grp")
    feature = node_feats.shape[1]
    slots_one = owner_one.shape[0]
    balance_one = slots_one // 2
    slots_two = owner_two.shape[0]
    me = lax.axis_index("grp").astype(jnp.int32).reshape(1)
    weights = (weight_in, weight_out, biases)

    cap_one = slots_one // groups
    prev, after = halo_pair(node_feats[:HALO], node_feats[-HALO:])
    near_two = gather_near(adjacency_two)
    message0, result0, sent_one, place_cols, mine_two = fine_forward(
        me, fine_columns, pool_one_columns, count_one, count_two, prev, after, owner_one.reshape(1, slots_one),
        owner_two.reshape(1, slots_two), columns_two, node_feats, fine_adjacency, pool_one, cotangent, *weights,
        groups, balance_one,
    )
    hops = sorted(near_two)
    sent_one, *near_two = lax.optimization_barrier((sent_one, *[near_two[hop] for hop in hops]))
    adj_two = gather_far(adjacency_two, dict(zip(hops, near_two)))
    first = exchange(sent_one)
    own_one = place_rows(first, balance_one)
    grad_up_one, gslots_two, table_one = place_pool(
        pool_two_columns, after_all(first, own_one), pool_two, balance_one, cap_one
    )
    at = 2 * cap_one + 2 + 2 * slots_two // 128
    columns_two_all = first[:, at : at + columns_two.shape[0], : columns_two.shape[1]].astype(jnp.int32)
    columns_two_all = columns_two_all.reshape(-1, columns_two.shape[1])
    message_one, result1, slots_two_mine = one_forward(
        me, columns_one, pool_two_columns, gather_hops(own_one), gslots_two, adjacency_one, pool_two,
        *weights,
    )
    level = 3 * feature
    up_send, gx_one, coarse_sums, *parts_back = coarse_levels(
        me, columns_two_all, columns_one, pool_two_columns, gather_hops(slots_two_mine), adj_two, mine_two, first,
        adjacency_one, pool_two, table_one, own_one, message_one, result1, grad_up_one,
        *weights, padded_rows(2 * level + 2),
    )
    grad_send = owner_sum(table_one, gx_one, scatter_hops(parts_back))
    grad_got = exchange(grad_send)
    up_got = exchange(after_all(up_send, grad_got))

    sum_rows = padded_rows(level + 1)
    gx_zero, gmsg_zero, sums_send = fine_grad(
        pool_one_columns, place_cols, grad_got, pool_one, coarse_sums, cotangent, node_feats, message0, *weights,
        sum_rows, lax.axis_size(ALL),
    )
    sums_send, up_got = lax.optimization_barrier((sums_send, up_got))
    shares = send_shares(sums_send)
    rim_low, rim_high, carry = spread_edge(fine_columns, fine_adjacency, gmsg_zero, gx_zero)
    from_prev, from_after = halo_pair(rim_low, rim_high)
    node_out = node_out_rows(pool_one_columns, place_cols, after_all(up_got, carry), pool_one, result0)
    shares, from_prev, from_after, node_out = lax.optimization_barrier((shares, from_prev, from_after, node_out))
    mine = jnp.sum(shares.astype(F32), axis=0).astype(BF)
    sums = share_sums(mine)
    from_prev = after_all(from_prev, mine)
    grad_feats = spread_inner(
        me, groups, fine_columns, fine_adjacency, gmsg_zero, gx_zero, carry, from_prev, from_after
    )
    scale = 1.0 / math.sqrt(node_feats.shape[0] * groups * lax.axis_size("slab"))
    return (node_out, grad_feats, *scaled_sums(sums, sum_rows // lax.axis_size(ALL), scale))


def solution(mesh):
    rows = P(("slab", "grp"), None)
    blocks = P(("slab", "grp"), None, None)
    flat = P(("slab", "grp"))
    placed = (
        rows, rows, blocks, rows, blocks, rows, flat, flat, blocks, rows,
        blocks, rows, flat, flat, blocks, rows, P(), P(), P(),
    )
    return jax.shard_map(
        body,
        mesh=mesh,
        in_specs=placed,
        out_specs=(rows, rows, P(), P(), P()),
        check_vma=False,
    )
```
